32 devices in a mesh: groups: 2 (over x), fsdp: 2 (over core), tp: 8 (over z, y).
Axes of the slice: x: 2, y: 2, z: 4, core: 2. Of those that a mesh axis runs over, the one named last changes fastest.
Arguments:
- hidden_in: bfloat16 [32, 8, 8192], P(('groups', 'fsdp')), parts along dimension 0, may hold values from -6 to 6
- input_gain: bfloat16 [8192], replicated, may hold values from 0.3984375 to 1.59375
- post_gain: bfloat16 [8192], replicated, may hold values from 0.3984375 to 1.59375
- query_base_weight: bfloat16 [8192, 8192], P('fsdp', 'tp'), may hold values from -6 to 6
- query_bias: bfloat16 [8192], P('tp'), may hold values from -5 to 5
- output_base_weight: bfloat16 [8192, 8192], P('tp', 'fsdp'), may hold values from -6 to 6
- query_lower_factor: bfloat16 [8192, 64], P(('fsdp', 'tp')), may hold values from -6 to 6
- query_upper_factor: bfloat16 [64, 8192], P('fsdp', 'tp'), may hold values from -0.75 to 0.75
- output_lower_factor: bfloat16 [8192, 64], P('tp', 'fsdp'), may hold values from -6 to 6
- output_upper_factor: bfloat16 [64, 8192], P(None, ('fsdp', 'tp')), may hold values from -0.75 to 0.75
- cache_keys: bfloat16 [32, 8, 2048, 128], P(('groups', 'fsdp'), 'tp'), parts along dimension 0, as said below
- cache_values: bfloat16 [32, 8, 2048, 128], P(('groups', 'fsdp'), 'tp'), parts along dimension 0, as said below
- cache_lengths: int32 [32], P(('groups', 'fsdp')), parts along dimension 0, may hold values from 512 to 2048, as said below
Outputs:
- residual_out: bfloat16 [32, 8, 8192], P(('groups', 'fsdp')), parts along dimension 0
- normed_out: bfloat16 [32, 8, 8192], P(('groups', 'fsdp')), parts along dimension 0
- query_effective: bfloat16 [16384, 8192], P(('groups', 'fsdp'), 'tp'), parts along dimension 0
- output_effective: bfloat16 [16384, 8192], P(('groups', 'tp'), 'fsdp'), parts along dimension 0
The draws below stay inside these ranges and needn't reach their ends.
There are 2 independent parts, one for each index of `groups`. The reference program is written for one: setup_inputs(seed, part) draws one part's arguments, and reference() takes and returns one part's arrays. A program takes and returns all parts, laid end to end along the dimension named above; an argument that names none is the same for every part. Nothing has to cross between parts.
Inputs may be any that keep to these rules, and one draw needn't show every extreme that they name: `cache_keys`: cache slots whose tp indices share a key head, that is whose index times 8 // 8 agree, hold equal keys. `cache_values`: laid out as cache_keys: slots sharing a value head hold equal values. `cache_lengths`: some row has exactly 2048 and some other row exactly 512.
All inputs are finite; a program needn't handle non-finite values.
Results may differ from the reference program's by a relative error of at most 0.006.
The reference program's roundings to bfloat16 on the way (of `normed`, `query`, `probs` and `context`) count: a program that leaves them out, or rounds other values in their place, can miss the bound.
Values may be sent and summed in bfloat16 or wider, within the bound.
No kernel may reach another device: no remote copies, remote signals or barrier semaphores. Data moves between devices by JAX's collectives and lax.ppermute only.
A program may use at most 192 MiB of HBM per device.

```python
import jax
import jax.numpy as jnp
from jax import lax

D = 8192
HEADS = 64
KVH = 8
HD = 128
RANK = 64
STEPS = 8
CTX = 2048
ROWS = 16
DQ = 8192
N_TP = 8


def cache_field(key, spread_factor):
    drawn = jax.random.normal(key, (ROWS, KVH, CTX, HD), jnp.float32)
    drawn = jnp.clip(drawn * spread_factor, -40.0, 40.0)
    return jnp.repeat(drawn, N_TP // KVH, axis=1).astype(jnp.bfloat16)


def draw_cache_keys(key, part):
    key = jax.random.fold_in(key, 11)
    return cache_field(key, 2.5)


def draw_cache_values(key, part):
    key = jax.random.fold_in(key, 23)
    return cache_field(key, 1.0)


def draw_cache_lengths(key, part):
    key = jax.random.fold_in(key, 37)
    drawn = jax.random.randint(key, (ROWS,), CTX // 4, CTX + 1, dtype=jnp.int32)
    first_key = jax.random.fold_in(key, 41)
    offset_key = jax.random.fold_in(key, 43)
    longest = jax.random.randint(first_key, (), 0, ROWS, dtype=jnp.int32)
    offset = jax.random.randint(offset_key, (), 1, ROWS, dtype=jnp.int32)
    shortest = (longest + offset) % ROWS
    places = jnp.arange(ROWS, dtype=jnp.int32)
    drawn = jnp.where(places == longest, jnp.int32(CTX), drawn)
    return jnp.where(places == shortest, jnp.int32(CTX // 4), drawn)


def spiked(array, rng, source, target, shards_of, factor):
    owner, partner = [(jnp.arange(array.shape[dim]) // (array.shape[dim] // shards_of)).reshape([-1 if axis == dim else 1 for axis in range(array.ndim)]) for dim in (source, target)]
    chosen = jax.random.permutation(rng, shards_of)[partner]
    strong = (owner == chosen) | (owner == (partner + shards_of // 2) % shards_of)
    return jnp.where(strong, factor * array, array)


def shard_levels(own_key, dims, split, low, top_value):
    level, own = 1.0, jax.random.fold_in(own_key, 6)
    for position, blocks in split:
        heights = jnp.exp(jax.random.uniform(jax.random.fold_in(own, position), (blocks,), jnp.float32, low / len(split), top_value / len(split)))
        level = level * jnp.repeat(heights, dims[position] // blocks).reshape([-1 if axis == position else 1 for axis in range(len(dims))])
    return level


def bell_draw(own_key, dims, scale, reach, shards=(), kind=jnp.bfloat16):
    values = jax.random.normal(own_key, dims, jnp.float32) * scale
    if len(shards) > 0:
        values = shard_levels(own_key, dims, shards, -0.22, 0.18) * values
    return jnp.clip(values, min=-reach, max=reach).astype(kind)


def gaussian_with(rng, extent, deviation, reach, shards, heavy, kind=jnp.bfloat16):
    values = deviation * jax.random.normal(rng, extent, jnp.float32)
    if shards:
        values = values * shard_levels(rng, extent, shards, -0.22, 0.18)
    return jnp.clip(spiked(values, jax.random.fold_in(rng, 3), *heavy), -reach, reach).astype(kind)


def setup_inputs(seed: int = 0, part: int = 0) -> dict:
    key_list = jax.random.split(jax.random.key(seed), 14)
    part_keys = jax.random.split(jax.random.fold_in(key_list[13], part), 14)
    return {
        "hidden_in": bell_draw(part_keys[0], (ROWS, STEPS, D), 1.0, 6.0, ((0, 2),)),
        "input_gain": jnp.clip(1.0 + 0.12 * jax.random.normal(key_list[1], (D,), jnp.float32), 0.3984375, 1.59375).astype(jnp.bfloat16),
        "post_gain": jnp.clip(1.0 + 0.12 * jax.random.normal(key_list[2], (D,), jnp.float32), 0.3984375, 1.59375).astype(jnp.bfloat16),
        "query_base_weight": bell_draw(key_list[3], (D, DQ), 1.0, 6.0, ((0, 2), (1, 8))),
        "query_bias": bell_draw(key_list[4], (DQ,), 1.0, 5.0, ((0, 8),)),
        "output_base_weight": gaussian_with(key_list[5], (DQ, D), 1.0, 6.0, ((0, 8), (1, 2)), (0, 1, 8, 2.0)),
        "query_lower_factor": bell_draw(key_list[6], (D, RANK), 1.0, 6.0, ((0, 16),)),
        "query_upper_factor": bell_draw(key_list[7], (RANK, DQ), RANK ** -0.5, 0.75, ((0, 2), (1, 8))),
        "output_lower_factor": bell_draw(key_list[8], (DQ, RANK), 1.0, 6.0, ((0, 8), (1, 2))),
        "output_upper_factor": bell_draw(key_list[9], (RANK, D), RANK ** -0.5, 0.75, ((1, 16),)),
        "cache_keys": draw_cache_keys(jax.random.fold_in(jax.random.fold_in(key_list[13], part), 71), part),
        "cache_values": draw_cache_values(jax.random.fold_in(jax.random.fold_in(key_list[13], part), 71), part),
        "cache_lengths": draw_cache_lengths(jax.random.fold_in(jax.random.fold_in(key_list[13], part), 71), part),
    }


NORM_EPS = 1e-06
ROPE_BASE = 1000000.0
ADAPTER_SCALE = 0.5

def rms_scale(values, gain):
    mean_square = lax.optimization_barrier(jnp.mean(values * values, axis=-1, keepdims=True))
    return values * lax.rsqrt(mean_square + NORM_EPS) * gain.astype(jnp.float32)

def rotate(query, lengths, steps):
    half = query.shape[-1] // 2
    inverse = ROPE_BASE ** (-(jnp.arange(half, dtype=jnp.float32) * 2.0) / query.shape[-1])
    positions = (lengths[:, None] - steps + jnp.arange(steps, dtype=jnp.int32)[None, :]).astype(jnp.float32)
    angles = positions[:, :, None, None] * inverse
    cosine = jnp.cos(angles)
    sine = jnp.sin(angles)
    first = query[..., :half]
    second = query[..., half:]
    return jnp.concatenate([first * cosine - second * sine, second * cosine + first * sine], axis=-1)

def reference(hidden_in, input_gain, post_gain, query_base_weight, query_bias, output_base_weight, query_lower_factor, query_upper_factor, output_lower_factor, output_upper_factor, cache_keys, cache_values, cache_lengths):
    query_effective = (query_base_weight.astype(jnp.float32) + ADAPTER_SCALE * jnp.dot(query_lower_factor, query_upper_factor, preferred_element_type=jnp.float32)).astype(jnp.bfloat16)
    output_effective = (output_base_weight.astype(jnp.float32) + ADAPTER_SCALE * jnp.dot(output_lower_factor, output_upper_factor, preferred_element_type=jnp.float32)).astype(jnp.bfloat16)
    inputs32 = hidden_in.astype(jnp.float32)
    normed = rms_scale(inputs32, input_gain).astype(jnp.bfloat16).reshape(ROWS * STEPS, D)
    query = jnp.dot(normed, query_effective, preferred_element_type=jnp.float32) * D ** (-0.5) + query_bias.astype(jnp.float32)
    query = rotate(query.reshape(ROWS, STEPS, HEADS, HD), cache_lengths, STEPS)
    query = (query * HD ** (-0.5)).astype(jnp.bfloat16)
    group = HEADS // KVH
    query = query.reshape(ROWS, STEPS, KVH, group, HD).astype(jnp.float32)
    stride = N_TP // KVH
    keys = cache_keys[:, ::stride].astype(jnp.float32)
    values = cache_values[:, ::stride].astype(jnp.float32)
    scores = jnp.einsum('rsgjd,rgkd->rgjsk', query, keys)
    limits = cache_lengths[:, None] - STEPS + jnp.arange(STEPS, dtype=jnp.int32)[None, :]
    allowed = jnp.arange(CTX, dtype=jnp.int32)[None, None, None, None, :] <= limits[:, None, None, :, None]
    scores = jnp.where(allowed, scores, jnp.float32(-1e+30))
    top = lax.optimization_barrier(jnp.max(scores, axis=-1, keepdims=True))
    weights = jnp.exp(scores - top)
    probs = (weights / lax.optimization_barrier(jnp.sum(weights, axis=-1, keepdims=True))).astype(jnp.bfloat16)
    context = jnp.einsum('rgjsk,rgkd->rsgjd', probs.astype(jnp.float32), values).astype(jnp.bfloat16)
    context = context.reshape(ROWS * STEPS, DQ)
    attended = jnp.dot(context, output_effective, preferred_element_type=jnp.float32).reshape(ROWS, STEPS, D) * DQ ** (-0.5)
    combined = inputs32 + attended
    return (combined.astype(jnp.bfloat16), rms_scale(combined, post_gain).astype(jnp.bfloat16), query_effective, output_effective)
```

```python
import functools

import jax
import jax.numpy as jnp
import numpy as np
from jax import lax
from jax.experimental import pallas as pl
from jax.experimental.pallas import tpu as pltpu
from jax.sharding import PartitionSpec as P

NORM_EPS = 1e-06
ROPE_BASE = 1000000.0
ADAPTER_SCALE = 0.5
VMEM_LIMIT = 32 * 1024 * 1024
BF16 = jnp.bfloat16
F16 = jnp.float16
F32 = jnp.float32
SWAP = [(0, 1), (1, 0)]


def params():
    return pltpu.CompilerParams(vmem_limit_bytes=VMEM_LIMIT)


def cost(flops, read):
    return pl.CostEstimate(flops=flops, bytes_accessed=read, transcendentals=0)


def hop(value, distance):
    total = lax.axis_size("tp")
    return lax.ppermute(value, "tp", [(i, i ^ distance) for i in range(total)])


def swap(value):
    return lax.ppermute(value, "fsdp", SWAP)


def contract_first(left, right):
    return lax.dot_general(left, right, (((0,), (0,)), ((), ())), preferred_element_type=F32)


def query_kernel(place, lower, upper, base, mine, theirs, effective, own, other):
    step = pl.program_id(0)

    @pl.when(step == 0)
    def _():
        own[...] = jnp.zeros_like(own)
        other[...] = jnp.zeros_like(other)

    update = contract_first(lower[0], upper[...])
    fresh = (base[...].astype(F32) + ADAPTER_SCALE * update).astype(BF16)
    effective[...] = fresh
    both = jnp.concatenate([mine[...], theirs[...]], axis=0)
    product = jnp.dot(both, fresh, preferred_element_type=F32)
    rows = own.shape[0]
    own[...] += product[:rows]
    other[...] += product[rows:]


def query_project(tp_index, lower, upper, base, mine, theirs):
    blocks, rank, depth = lower.shape
    width = base.shape[1]
    rows = mine.shape[0]
    spec = pltpu.PrefetchScalarGridSpec(
        num_scalar_prefetch=1,
        grid=(blocks,),
        in_specs=[
            pl.BlockSpec((1, rank, depth), lambda k, t: (k, 0, 0)),
            pl.BlockSpec((rank, width), lambda k, t: (0, 0)),
            pl.BlockSpec((depth, width), lambda k, t: (k ^ t[0], 0)),
            pl.BlockSpec((rows, depth), lambda k, t: (0, k ^ t[0])),
            pl.BlockSpec((rows, depth), lambda k, t: (0, k ^ t[0])),
        ],
        out_specs=[
            pl.BlockSpec((depth, width), lambda k, t: (k ^ t[0], 0)),
            pl.BlockSpec((rows, width), lambda k, t: (0, 0)),
            pl.BlockSpec((rows, width), lambda k, t: (0, 0)),
        ],
    )
    return pl.pallas_call(
        query_kernel,
        grid_spec=spec,
        out_shape=[
            jax.ShapeDtypeStruct(base.shape, BF16),
            jax.ShapeDtypeStruct((rows, width), F32),
            jax.ShapeDtypeStruct((rows, width), F32),
        ],
        compiler_params=params(),
        cost_estimate=cost(2 * base.size * (rank + 2 * rows), 4 * base.size),
        name="query_project",
    )(tp_index, lower, upper, base, mine, theirs)


def attend_kernel(steps, heads, head_dim, scale, lengths, own, other, bias, cosine, sine, keys, values, context):
    group = keys.shape[0]
    slots = keys.shape[1]
    first = pl.program_id(0) * group
    query = (own[...] + other[...]) * scale + bias[...].astype(F32)
    turned = []
    for head in range(heads):
        part = query[:, head * head_dim : (head + 1) * head_dim]
        part = part * cosine[...] + pltpu.roll(part, head_dim // 2, 1) * sine[...]
        turned.append(part * head_dim ** (-0.5))
    slot = lax.broadcasted_iota(jnp.int32, (heads * steps, slots), 1)
    step = lax.broadcasted_iota(jnp.int32, (heads * steps, slots), 0) % steps
    gathered = []
    for row in range(group):
        rows = jnp.concatenate([q[row * steps : (row + 1) * steps] for q in turned], axis=0).astype(BF16)
        scores = lax.dot_general(
            rows, keys[row], (((1,), (1,)), ((), ())), preferred_element_type=F32
        )
        scores = jnp.where(slot - step <= lengths[first + row] - steps, scores, F32(-1e30))
        top = jnp.max(scores, axis=-1, keepdims=True)
        weights = jnp.exp(scores - top)
        probs = (weights / jnp.sum(weights, axis=-1, keepdims=True)).astype(BF16)
        gathered.append(jnp.dot(probs, values[row], preferred_element_type=F32))
    for head in range(heads):
        context[:, head * head_dim : (head + 1) * head_dim] = jnp.concatenate(
            [g[head * steps : (head + 1) * steps] for g in gathered], axis=0
        ).astype(BF16)


def attend(lengths, own, other, bias, cosine, sine, keys, values, steps, scale):
    rows, slots, head_dim = keys.shape
    width = own.shape[1]
    heads = width // head_dim
    group = 2
    tall = group * steps
    spec = pltpu.PrefetchScalarGridSpec(
        num_scalar_prefetch=1,
        grid=(rows // group,),
        in_specs=[
            pl.BlockSpec((tall, width), lambda r, n: (r, 0)),
            pl.BlockSpec((tall, width), lambda r, n: (r, 0)),
            pl.BlockSpec((1, width), lambda r, n: (0, 0)),
            pl.BlockSpec((tall, head_dim), lambda r, n: (r, 0)),
            pl.BlockSpec((tall, head_dim), lambda r, n: (r, 0)),
            pl.BlockSpec((group, slots, head_dim), lambda r, n: (r, 0, 0)),
            pl.BlockSpec((group, slots, head_dim), lambda r, n: (r, 0, 0)),
        ],
        out_specs=pl.BlockSpec((tall, width), lambda r, n: (r, 0)),
    )
    return pl.pallas_call(
        functools.partial(attend_kernel, steps, heads, head_dim, scale),
        grid_spec=spec,
        out_shape=jax.ShapeDtypeStruct((rows * steps, width), BF16),
        compiler_params=params(),
        cost_estimate=cost(4 * keys.size * heads * steps, 4 * keys.size),
        name="attend",
    )(lengths, own, other, bias, cosine, sine, keys, values)


def output_kernel(place, lower, upper, base, mine, theirs, effective, own, other):
    update = contract_first(lower[...], upper[0])
    fresh = (base[...].astype(F32) + ADAPTER_SCALE * update).astype(BF16)
    effective[...] = fresh
    both = jnp.concatenate([mine[...], theirs[...]], axis=0)
    product = jnp.dot(both, fresh, preferred_element_type=F32)
    rows = mine.shape[0]
    own[0, 0] = product[:rows]
    other[0, 0] = product[rows:]


def output_project(tp_index, lower, upper, base, mine, theirs):
    blocks = lax.axis_size("tp")
    depth, whole = base.shape
    width = whole // blocks
    rank = lower.shape[0]
    rows = mine.shape[0]
    spec = pltpu.PrefetchScalarGridSpec(
        num_scalar_prefetch=1,
        grid=(blocks,),
        in_specs=[
            pl.BlockSpec((rank, depth), lambda k, t: (0, 0)),
            pl.BlockSpec((1, rank, width), lambda k, t: (k, 0, 0)),
            pl.BlockSpec((depth, width), lambda k, t: (0, k ^ t[0])),
            pl.BlockSpec((rows, depth), lambda k, t: (0, 0)),
            pl.BlockSpec((rows, depth), lambda k, t: (0, 0)),
        ],
        out_specs=[
            pl.BlockSpec((depth, width), lambda k, t: (0, k ^ t[0])),
            pl.BlockSpec((1, 1, rows, width), lambda k, t: (k % 2, k // 2, 0, 0)),
            pl.BlockSpec((1, 1, rows, width), lambda k, t: (k // 2, k % 2, 0, 0)),
        ],
    )
    return pl.pallas_call(
        output_kernel,
        grid_spec=spec,
        out_shape=[
            jax.ShapeDtypeStruct(base.shape, BF16),
            jax.ShapeDtypeStruct((2, blocks // 2, rows, width), F32),
            jax.ShapeDtypeStruct((blocks // 2, 2, rows, width), F32),
        ],
        compiler_params=params(),
        cost_estimate=cost(2 * base.size * (rank + 2 * rows), 4 * base.size),
        name="output_project",
    )(tp_index, lower, upper, base, mine, theirs)


def finish_kernel(place, bound, hidden, gain, near, far, residual, normed, combined):
    blocks, rows, width = near.shape
    half = blocks * width
    squares = jnp.zeros((rows, 1), F32)
    for pieces, which in ((near, place[1]), (far, 1 - place[1])):
        for k in range(blocks):
            start = pl.multiple_of(which * half + (place[0] ^ k) * width, width)
            total = hidden[:, pl.ds(start, width)].astype(F32) + pieces[k] * bound[0]
            combined[:, pl.ds(start, width)] = total
            residual[:, pl.ds(start, width)] = total.astype(BF16)
            squares += jnp.sum(total * total, axis=-1, keepdims=True)
    inverse = lax.rsqrt(squares / (2 * half) + NORM_EPS)
    normed[...] = (combined[...] * inverse * gain[...].astype(F32)).astype(BF16)


def finish(place, bound, hidden, gain, near, far):
    rows, whole = hidden.shape
    blocks, _, width = near.shape
    tall = 16
    spec = pltpu.PrefetchScalarGridSpec(
        num_scalar_prefetch=2,
        grid=(rows // tall,),
        in_specs=[
            pl.BlockSpec((tall, whole), lambda r, p, b: (r, 0)),
            pl.BlockSpec((1, whole), lambda r, p, b: (0, 0)),
            pl.BlockSpec((blocks, tall, width), lambda r, p, b: (0, r, 0)),
            pl.BlockSpec((blocks, tall, width), lambda r, p, b: (0, r, 0)),
        ],
        out_specs=[
            pl.BlockSpec((tall, whole), lambda r, p, b: (r, 0)),
            pl.BlockSpec((tall, whole), lambda r, p, b: (r, 0)),
        ],
        scratch_shapes=[pltpu.VMEM((tall, whole), F32)],
    )
    return pl.pallas_call(
        finish_kernel,
        grid_spec=spec,
        out_shape=[jax.ShapeDtypeStruct((rows, whole), BF16)] * 2,
        compiler_params=params(),
        cost_estimate=cost(8 * hidden.size, 14 * hidden.size),
        name="finish",
    )(place, bound, hidden, gain, near, far)


def gather_blocks(value):
    outer = lax.axis_size("tp") // 2
    cut = value.shape[0] // 2
    low, high = value[:cut], value[cut:]
    pair = jnp.stack([high, hop(high, 1)])
    along = jnp.stack([low] + [hop(low, 2 * k) for k in range(1, outer)])
    pairs = jnp.stack([pair] + [hop(pair, 2 * k) for k in range(1, outer)])
    lows = jnp.stack([along, hop(along, 1)], axis=1)
    both = jnp.concatenate([lows, pairs], axis=2)
    return both.reshape((2 * outer,) + value.shape)


def reduce_blocks(own, other, shrink):
    outer = other.shape[0]

    def narrow(value):
        return value.astype(F16)

    across = hop(narrow(shrink(own[1])), 1)
    arrived = [hop(narrow(shrink(other[k])), 2 * k) for k in range(1, outer)]
    summed = shrink(own[0]) + across.astype(F32)
    pair = shrink(other[0]) + sum(a.astype(F32) for a in arrived)
    rest = hop(narrow(pair[1]), 1)
    total = summed[0] + sum(hop(narrow(summed[k]), 2 * k).astype(F32) for k in range(1, outer))
    return narrow(total), narrow(pair[0] + rest.astype(F32))


def local(
    hidden_in,
    input_gain,
    post_gain,
    query_base_weight,
    query_bias,
    output_base_weight,
    query_lower_factor,
    query_upper_factor,
    output_lower_factor,
    output_upper_factor,
    cache_keys,
    cache_values,
    cache_lengths,
):
    rows, steps, width = hidden_in.shape
    tall = rows * steps
    half = width // 2
    slots, head_dim = cache_keys.shape[2:]
    features = query_base_weight.shape[1] * lax.axis_size("tp")
    t = lax.axis_index("tp").astype(jnp.int32)
    f = lax.axis_index("fsdp").astype(jnp.int32)
    place = jnp.stack([t, f])
    outer = lax.axis_size("tp") // 2

    lower = gather_blocks(query_lower_factor.T)

    flat = hidden_in.reshape(tall, width)
    inputs32 = flat.astype(F32)
    mean_square = jnp.mean(inputs32 * inputs32, axis=-1, keepdims=True)
    normed = (inputs32 * lax.rsqrt(mean_square + NORM_EPS) * input_gain.astype(F32)).astype(BF16)
    mine = lax.dynamic_slice_in_dim(normed, f * half, half, 1)
    theirs = swap(lax.dynamic_slice_in_dim(normed, (1 - f) * half, half, 1))

    reach = jnp.arange(slots, dtype=jnp.int32)[None, :, None] < cache_lengths[:, None, None]
    bound = jnp.max(jnp.where(reach, jnp.abs(cache_values[:, 0].astype(F32)), 0.0)).astype(BF16)
    rank_part = query_upper_factor.shape[0]
    lower_o = output_lower_factor.T
    columns = query_upper_factor.shape[1]
    sent = jnp.concatenate(
        [query_upper_factor, lower_o, jnp.broadcast_to(bound, (16, columns))], axis=0
    )
    came = swap(sent)

    def in_order(a, b):
        return jnp.where(f == 0, jnp.concatenate([a, b]), jnp.concatenate([b, a]))

    upper = in_order(sent[:rank_part], came[:rank_part])
    lower_o = in_order(sent[rank_part : 2 * rank_part], came[rank_part : 2 * rank_part])
    bound = jnp.maximum(sent[2 * rank_part :], came[2 * rank_part :])

    rank = output_upper_factor.shape[0]
    block = output_upper_factor.shape[1]
    message = jnp.concatenate([output_upper_factor, bound[:, :block]], axis=0)
    message, lower = lax.optimization_barrier((message, lower))
    message = jnp.concatenate([message, message[-16:]], axis=0)
    gathered = gather_blocks(message)
    upper_o = gathered[:, :rank]
    bound = jnp.max(gathered[:, rank:]).astype(F32)

    query_effective, own, other = query_project(
        t[None], lower, upper, query_base_weight, mine, theirs
    )
    other = swap(other)

    inverse = ROPE_BASE ** (-(np.arange(head_dim // 2) * 2.0) / head_dim)
    inverse = jnp.asarray(inverse.astype(np.float32))
    positions = cache_lengths[:, None] - steps + jnp.arange(steps, dtype=jnp.int32)[None, :]
    angles = positions.astype(F32).reshape(tall, 1) * inverse
    cosine, sine = jnp.cos(angles), jnp.sin(angles)
    context = attend(
        cache_lengths,
        own,
        other,
        query_bias[None, :],
        jnp.concatenate([cosine, cosine], axis=1),
        jnp.concatenate([-sine, sine], axis=1),
        cache_keys[:, 0],
        cache_values[:, 0],
        steps,
        width ** (-0.5),
    )

    output_effective, own, other = output_project(
        t[None], lower_o, upper_o, output_base_weight, context, swap(context)
    )

    small = 2.0**-16
    unit = jnp.maximum(bound, 1e-30) * small
    shrink_by = 1.0 / unit

    def shrink(value):
        return (value * shrink_by) * (features ** (-0.5) * small)

    near, far = reduce_blocks(own, other, shrink)
    far = swap(far)

    along = jnp.stack([near] + [hop(near, 2 * k) for k in range(1, outer)])
    pair = jnp.stack([far, hop(far, 1)])
    pairs = jnp.stack([pair] + [hop(pair, 2 * k) for k in range(1, outer)])
    near = jnp.stack([along, hop(along, 1)], axis=1)
    near = near.reshape((2 * outer,) + near.shape[2:]).astype(F32)
    far = pairs.reshape((2 * outer,) + pairs.shape[2:]).astype(F32)

    residual, normed_out = finish(
        place, jnp.maximum(bound, 1e-30)[None], flat, post_gain[None, :], near, far
    )
    return (
        residual.reshape(hidden_in.shape),
        normed_out.reshape(hidden_in.shape),
        query_effective,
        output_effective,
    )


def solution(mesh):
    in_specs = (
        P(("groups", "fsdp"), None, None),
        P(),
        P(),
        P("fsdp", "tp"),
        P("tp"),
        P("tp", "fsdp"),
        P(("fsdp", "tp"), None),
        P("fsdp", "tp"),
        P("tp", "fsdp"),
        P(None, ("fsdp", "tp")),
        P(("groups", "fsdp"), "tp", None, None),
        P(("groups", "fsdp"), "tp", None, None),
        P(("groups", "fsdp")),
    )
    out_specs = (
        P(("groups", "fsdp"), None, None),
        P(("groups", "fsdp"), None, None),
        P(("groups", "fsdp"), "tp"),
        P(("groups", "tp"), "fsdp"),
    )
    return jax.shard_map(local, mesh=mesh, in_specs=in_specs, out_specs=out_specs, check_vma=False)
```

```python
import functools

import jax
import jax.numpy as jnp
import numpy as np
from jax import lax
from jax.experimental import pallas as pl
from jax.experimental.pallas import tpu as pltpu
from jax.sharding import PartitionSpec as P

NORM_EPS = 1e-06
ROPE_BASE = 1000000.0
ADAPTER_SCALE = 0.5
MIB = 1024 * 1024
BF16 = jnp.bfloat16
F16 = jnp.float16
F32 = jnp.float32
SWAP = [(0, 1), (1, 0)]


def params(room):
    return pltpu.CompilerParams(vmem_limit_bytes=room * MIB)


def cost(flops, read):
    return pl.CostEstimate(flops=flops, bytes_accessed=read, transcendentals=0)


def hop(value, distance):
    total = lax.axis_size("tp")
    return lax.ppermute(value, "tp", [(i, i ^ distance) for i in range(total)])


def swap(value):
    return lax.ppermute(value, "fsdp", SWAP)


def contract_first(left, right):
    return lax.dot_general(left, right, (((0,), (0,)), ((), ())), preferred_element_type=F32)


VMEM = pl.BlockSpec(memory_space=pltpu.VMEM)
SMEM = pl.BlockSpec(memory_space=pltpu.SMEM)
ANY = pl.BlockSpec(memory_space=pl.ANY)


def in_vmem(value):
    return pltpu.with_memory_space_constraint(value, pltpu.VMEM)


def in_hbm(value):
    return pltpu.with_memory_space_constraint(value, pltpu.HBM)


def fetch_kernel(source, target, arrived):
    copy = pltpu.make_async_copy(source, target, arrived)
    copy.start()
    copy.wait()


def fetch(value, name):
    return pl.pallas_call(
        fetch_kernel,
        in_specs=[ANY],
        out_specs=VMEM,
        out_shape=pltpu.VMEM(value.shape, value.dtype),
        scratch_shapes=[pltpu.SemaphoreType.DMA],
        compiler_params=params(2),
        cost_estimate=cost(0, 2 * value.size),
        name=name,
    )(in_hbm(value))


def reach_kernel(lengths, values, bound, held, arrived):
    rows, slots, head_dim = values.shape
    copies = [
        pltpu.make_async_copy(values.at[row], held.at[row], arrived.at[row]) for row in range(rows)
    ]
    for copy in copies:
        copy.start()
    slot = lax.broadcasted_iota(jnp.int32, (slots, head_dim), 0)
    top = jnp.zeros((8, head_dim), F32)
    for row in range(rows):
        copies[row].wait()
        size = jnp.where(slot < lengths[row], jnp.abs(held[row].astype(F32)), 0.0)
        top = jnp.maximum(top, jnp.max(size.reshape(-1, 8, head_dim), axis=0))
    bound[...] = jnp.broadcast_to(jnp.max(top), bound.shape).astype(BF16)


def largest_in_reach(lengths, values, columns):
    return pl.pallas_call(
        reach_kernel,
        in_specs=[SMEM, ANY],
        out_specs=VMEM,
        out_shape=jax.ShapeDtypeStruct((16, columns), BF16),
        scratch_shapes=[
            pltpu.VMEM(values.shape, BF16),
            pltpu.SemaphoreType.DMA((values.shape[0],)),
        ],
        compiler_params=params(8),
        cost_estimate=cost(4 * values.size, 2 * values.size),
        name="largest_in_reach",
    )(lengths, in_hbm(values))


def query_kernel(
    place, near, far, upper, base, mine, theirs, effective, own, other, fresh, total, left
):
    outer, _, depth = near.shape
    rows = mine.shape[0]
    total[...] = jnp.zeros_like(total)

    def pair(z, _):
        for y, lower in ((0, near), (1, far)):
            start = pl.multiple_of(((2 * z + y) ^ place[0]) * depth, depth)
            block = pl.ds(start, depth)
            out = pltpu.make_async_copy(fresh.at[y], effective.at[block], left.at[y])

            @pl.when(z > 0)
            def _():
                out.wait()

            update = contract_first(lower[z], upper[...])
            fresh[y] = (base[block, :].astype(F32) + update).astype(BF16)
            out.start()
            both = jnp.concatenate([mine[:, block], theirs[:, block]], axis=0)
            total[...] += jnp.dot(both, fresh[y], preferred_element_type=F32)
        return 0

    lax.fori_loop(0, outer, pair, 0)
    own[...] = total[:rows]
    other[...] = total[rows:]
    for y in range(2):
        pltpu.make_async_copy(fresh.at[y], effective.at[pl.ds(0, depth)], left.at[y]).wait()


def query_project(place, near, far, upper, base, mine, theirs):
    depth = near.shape[2]
    width = base.shape[1]
    rows = mine.shape[0]
    return pl.pallas_call(
        query_kernel,
        in_specs=[SMEM] + [VMEM] * 6,
        out_specs=[ANY, VMEM, VMEM],
        out_shape=[
            jax.ShapeDtypeStruct(base.shape, BF16),
            jax.ShapeDtypeStruct((rows, width), F32),
            jax.ShapeDtypeStruct((rows, width), F32),
        ],
        scratch_shapes=[
            pltpu.VMEM((2, depth, width), BF16),
            pltpu.VMEM((2 * rows, width), F32),
            pltpu.SemaphoreType.DMA((2,)),
        ],
        compiler_params=params(14),
        cost_estimate=cost(2 * base.size * (near.shape[1] + 2 * rows), 2 * base.size),
        name="query_project",
    )(place, near, far, upper, in_vmem(base), mine, theirs)


def attend_kernel(
    steps, scale, lengths, own, other, bias, cosine, sine, keys, values, context,
    keys_held, values_held, arrived
):
    rows, slots, head_dim = keys.shape
    heads = own.shape[1] // head_dim
    group = 2
    copies = []
    for row in range(rows):
        copies.append(
            [
                pltpu.make_async_copy(keys.at[row], keys_held.at[row], arrived.at[0, row]),
                pltpu.make_async_copy(values.at[row], values_held.at[row], arrived.at[1, row]),
            ]
        )
        for copy in copies[row]:
            copy.start()
    slot = lax.broadcasted_iota(jnp.int32, (heads * steps, slots), 1)
    step = lax.broadcasted_iota(jnp.int32, (heads * steps, slots), 0) % steps
    behind = slot - step
    for first in range(0, rows, group):
        span = slice(first * steps, (first + group) * steps)
        query = (own[span] + other[span]) * scale + bias[...].astype(F32)
        turned = []
        for head in range(heads):
            part = query[:, head * head_dim : (head + 1) * head_dim]
            part = part * cosine[span] + pltpu.roll(part, head_dim // 2, 1) * sine[span]
            turned.append(part * head_dim ** (-0.5))
        gathered = []
        for row in range(group):
            for copy in copies[first + row]:
                copy.wait()
            queries = jnp.concatenate(
                [q[row * steps : (row + 1) * steps] for q in turned], axis=0
            ).astype(BF16)
            scores = lax.dot_general(
                queries,
                keys_held[first + row],
                (((1,), (1,)), ((), ())),
                preferred_element_type=F32,
            )
            scores = jnp.where(behind <= lengths[first + row] - steps, scores, F32(-1e30))
            top = jnp.max(scores, axis=-1, keepdims=True)
            weights = jnp.exp(scores - top)
            probs = (weights / jnp.sum(weights, axis=-1, keepdims=True)).astype(BF16)
            gathered.append(
                jnp.dot(probs, values_held[first + row], preferred_element_type=F32)
            )
        for head in range(heads):
            context[span, head * head_dim : (head + 1) * head_dim] = jnp.concatenate(
                [g[head * steps : (head + 1) * steps] for g in gathered], axis=0
            ).astype(BF16)


def attend(lengths, own, other, bias, cosine, sine, keys, values, steps, scale):
    rows = keys.shape[0]
    width = own.shape[1]
    return pl.pallas_call(
        functools.partial(attend_kernel, steps, scale),
        in_specs=[SMEM] + [VMEM] * 5 + [ANY] * 2,
        out_specs=VMEM,
        out_shape=jax.ShapeDtypeStruct((rows * steps, width), BF16),
        scratch_shapes=[
            pltpu.VMEM(keys.shape, BF16),
            pltpu.VMEM(values.shape, BF16),
            pltpu.SemaphoreType.DMA((2, rows)),
        ],
        compiler_params=params(18),
        cost_estimate=cost(4 * keys.size * width // keys.shape[2] * steps, 4 * keys.size),
        name="attend",
    )(lengths, own, other, bias, cosine, sine, in_hbm(keys), in_hbm(values))


def output_kernel(
    place, lower, upper, base, mine, theirs, effective, own, other, held, fresh, arrived, left
):
    outer = upper.shape[0]
    rank = lower.shape[0]
    width = upper.shape[3]
    rows = mine.shape[0]

    def columns(k):
        return pl.ds(pl.multiple_of((k ^ place[0]) * width, width), width)

    def fetch(k):
        return pltpu.make_async_copy(base.at[:, columns(k)], held.at[k], arrived.at[k])

    def ask(k, _):
        fetch(k).start()
        return 0

    lax.fori_loop(0, 2 * outer, ask, 0)
    both = jnp.concatenate([mine[...], theirs[...]], axis=0)

    def pair(z, _):
        for y in range(2):
            k = 2 * z + y
            out = pltpu.make_async_copy(fresh.at[y], effective.at[:, columns(k)], left.at[y])

            @pl.when(z > 0)
            def _():
                out.wait()

            update = contract_first(lower[...], upper[z, y, :rank])
            fetch(k).wait()
            fresh[y] = (held[k].astype(F32) + update).astype(BF16)
            out.start()
            product = jnp.dot(both, fresh[y], preferred_element_type=F32)
            own[y, z] = product[:rows]
            other[z, y] = product[rows:]
        return 0

    lax.fori_loop(0, outer, pair, 0)
    for y in range(2):
        pltpu.make_async_copy(fresh.at[y], effective.at[:, pl.ds(0, width)], left.at[y]).wait()


def output_project(place, lower, upper, base, mine, theirs):
    outer = upper.shape[0]
    width = upper.shape[3]
    depth = base.shape[0]
    rows = mine.shape[0]
    return pl.pallas_call(
        output_kernel,
        in_specs=[SMEM, VMEM, VMEM, ANY, VMEM, VMEM],
        out_specs=[ANY, VMEM, VMEM],
        out_shape=[
            jax.ShapeDtypeStruct(base.shape, BF16),
            jax.ShapeDtypeStruct((2, outer, rows, width), F32),
            jax.ShapeDtypeStruct((outer, 2, rows, width), F32),
        ],
        scratch_shapes=[
            pltpu.VMEM((2 * outer, depth, width), BF16),
            pltpu.VMEM((2, depth, width), BF16),
            pltpu.SemaphoreType.DMA((2 * outer,)),
            pltpu.SemaphoreType.DMA((2,)),
        ],
        compiler_params=params(24),
        cost_estimate=cost(2 * base.size * (lower.shape[0] + 2 * rows), 4 * base.size),
        name="output_project",
    )(place, lower, upper, in_hbm(base), mine, theirs)


def finish_kernel(place, bound, hidden, gain, near, far, residual, normed, combined):
    blocks, rows, width = near.shape
    half = blocks * width
    squares = jnp.zeros((rows, 1), F32)
    for pieces, which in ((near, place[1]), (far, 1 - place[1])):
        for k in range(blocks):
            start = pl.multiple_of(which * half + (place[0] ^ k) * width, width)
            total = hidden[:, pl.ds(start, width)].astype(F32) + pieces[k] * bound[0]
            combined[:, pl.ds(start, width)] = total
            residual[:, pl.ds(start, width)] = total.astype(BF16)
            squares += jnp.sum(total * total, axis=-1, keepdims=True)
    inverse = lax.rsqrt(squares / (2 * half) + NORM_EPS)
    normed[...] = (combined[...] * inverse * gain[...].astype(F32)).astype(BF16)


def finish(place, bound, hidden, gain, near, far):
    rows, whole = hidden.shape
    blocks, _, width = near.shape
    tall = 16
    spec = pltpu.PrefetchScalarGridSpec(
        num_scalar_prefetch=2,
        grid=(rows // tall,),
        in_specs=[
            pl.BlockSpec((tall, whole), lambda r, p, b: (r, 0)),
            pl.BlockSpec((1, whole), lambda r, p, b: (0, 0)),
            pl.BlockSpec((blocks, tall, width), lambda r, p, b: (0, r, 0)),
            pl.BlockSpec((blocks, tall, width), lambda r, p, b: (0, r, 0)),
        ],
        out_specs=[
            pl.BlockSpec((tall, whole), lambda r, p, b: (r, 0)),
            pl.BlockSpec((tall, whole), lambda r, p, b: (r, 0)),
        ],
        scratch_shapes=[pltpu.VMEM((tall, whole), F32)],
    )
    return pl.pallas_call(
        finish_kernel,
        grid_spec=spec,
        out_shape=[jax.ShapeDtypeStruct((rows, whole), BF16)] * 2,
        compiler_params=params(14),
        cost_estimate=cost(8 * hidden.size, 14 * hidden.size),
        name="finish",
    )(place, bound, hidden, gain, near, far)


def cross(value):
    total = lax.axis_size("tp")
    pairs = [(f * total + i, (1 - f) * total + (i ^ 1)) for f in range(2) for i in range(total)]
    return lax.ppermute(value, ("fsdp", "tp"), pairs)


def along_z(value):
    outer = lax.axis_size("tp") // 2
    return jnp.stack([value] + [hop(value, 2 * k) for k in range(1, outer)])


def along_y(value):
    return jnp.stack([value, hop(value, 1)])


def reduce_blocks(own, other, shrink):
    outer = other.shape[0]

    def narrow(value):
        return value.astype(F16)

    across = hop(narrow(shrink(own[1])), 1)
    arrived = [hop(narrow(shrink(other[k])), 2 * k) for k in range(1, outer)]
    summed = shrink(own[0]) + across.astype(F32)
    ended = [hop(narrow(summed[k]), 2 * k) for k in range(1, outer)]
    arrived, ended = lax.optimization_barrier((arrived, ended))
    total = summed[0] + sum(e.astype(F32) for e in ended)
    pair = narrow(shrink(other[0]) + sum(a.astype(F32) for a in arrived))
    far = swap(pair[0]).astype(F32) + cross(pair[1]).astype(F32)
    return narrow(total), narrow(far)


def local(
    hidden_in,
    input_gain,
    post_gain,
    query_base_weight,
    query_bias,
    output_base_weight,
    query_lower_factor,
    query_upper_factor,
    output_lower_factor,
    output_upper_factor,
    cache_keys,
    cache_values,
    cache_lengths,
):
    rows, steps, width = hidden_in.shape
    tall = rows * steps
    half = width // 2
    slots, head_dim = cache_keys.shape[2:]
    features = query_base_weight.shape[1] * lax.axis_size("tp")
    t = lax.axis_index("tp").astype(jnp.int32)
    f = lax.axis_index("fsdp").astype(jnp.int32)
    place = jnp.stack([t, f])
    outer = lax.axis_size("tp") // 2

    lower_near = along_z(query_lower_factor.T)
    lower_far = hop(lower_near, 1)

    flat = hidden_in.reshape(tall, width)
    inputs32 = flat.astype(F32)
    mean_square = jnp.mean(inputs32 * inputs32, axis=-1, keepdims=True)
    normed = (inputs32 * lax.rsqrt(mean_square + NORM_EPS) * input_gain.astype(F32)).astype(BF16)
    mine = lax.dynamic_slice_in_dim(normed, f * half, half, 1)
    theirs = swap(lax.dynamic_slice_in_dim(normed, (1 - f) * half, half, 1))

    columns = query_upper_factor.shape[1]
    bound = largest_in_reach(cache_lengths, cache_values[:, 0], columns)
    rank_part = query_upper_factor.shape[0]
    sent = jnp.concatenate([query_upper_factor, output_lower_factor.T, bound], axis=0)
    came = swap(sent)

    def in_order(a, b):
        return jnp.where(f == 0, jnp.concatenate([a, b]), jnp.concatenate([b, a]))

    upper = in_order(sent[:rank_part], came[:rank_part]) * BF16(ADAPTER_SCALE)
    lower_o = in_order(sent[rank_part : 2 * rank_part], came[rank_part : 2 * rank_part])
    lower_o = lower_o * BF16(ADAPTER_SCALE)
    bound = jnp.maximum(sent[2 * rank_part :], came[2 * rank_part :])

    rank, block = output_upper_factor.shape
    message = jnp.concatenate([output_upper_factor, bound[:, :block]], axis=0)
    upper_o = along_z(along_y(message))
    bound = jnp.max(upper_o[:, :, rank:]).astype(F32)

    weight_q, _ = lax.optimization_barrier((query_base_weight, lower_near))
    query_effective, own, other = query_project(
        t[None], lower_near, lower_far, upper, fetch(weight_q, "fetch_query"), mine, theirs
    )
    other = swap(other)

    inverse = ROPE_BASE ** (-(np.arange(head_dim // 2) * 2.0) / head_dim)
    inverse = jnp.asarray(inverse.astype(np.float32))
    positions = cache_lengths[:, None] - steps + jnp.arange(steps, dtype=jnp.int32)[None, :]
    angles = positions.astype(F32).reshape(tall, 1) * inverse
    cosine, sine = jnp.cos(angles), jnp.sin(angles)
    context = attend(
        cache_lengths,
        own,
        other,
        query_bias[None, :],
        jnp.concatenate([cosine, cosine], axis=1),
        jnp.concatenate([-sine, sine], axis=1),
        cache_keys[:, 0],
        cache_values[:, 0],
        steps,
        width ** (-0.5),
    )

    output_effective, own, other = output_project(
        t[None], lower_o, upper_o, output_base_weight, context, swap(context)
    )

    small = 2.0**-16
    unit = jnp.maximum(bound, 1e-30) * small
    shrink_by = 1.0 / unit

    def shrink(value):
        return (value * shrink_by) * (features ** (-0.5) * small)

    near, far = reduce_blocks(own, other, shrink)

    near = along_z(near)
    near = jnp.stack([near, hop(near, 1)], axis=1)
    far = along_z(along_y(far))
    near = near.reshape((2 * outer,) + near.shape[2:]).astype(F32)
    far = far.reshape((2 * outer,) + far.shape[2:]).astype(F32)

    residual, normed_out = finish(
        place, jnp.maximum(bound, 1e-30)[None], flat, post_gain[None, :], near, far
    )
    return (
        residual.reshape(hidden_in.shape),
        normed_out.reshape(hidden_in.shape),
        query_effective,
        output_effective,
    )


def solution(mesh):
    in_specs = (
        P(("groups", "fsdp"), None, None),
        P(),
        P(),
        P("fsdp", "tp"),
        P("tp"),
        P("tp", "fsdp"),
        P(("fsdp", "tp"), None),
        P("fsdp", "tp"),
        P("tp", "fsdp"),
        P(None, ("fsdp", "tp")),
        P(("groups", "fsdp"), "tp", None, None),
        P(("groups", "fsdp"), "tp", None, None),
        P(("groups", "fsdp")),
    )
    out_specs = (
        P(("groups", "fsdp"), None, None),
        P(("groups", "fsdp"), None, None),
        P(("groups", "fsdp"), "tp"),
        P(("groups", "tp"), "fsdp"),
    )
    return jax.shard_map(local, mesh=mesh, in_specs=in_specs, out_specs=out_specs, check_vma=False)
```

```python
import functools

import jax
import jax.numpy as jnp
import numpy as np
from jax import lax
from jax.experimental import pallas as pl
from jax.experimental.pallas import tpu as pltpu
from jax.sharding import PartitionSpec as P

NORM_EPS = 1e-06
ROPE_BASE = 1000000.0
ADAPTER_SCALE = 0.5
MIB = 1024 * 1024
BF16 = jnp.bfloat16
F16 = jnp.float16
F32 = jnp.float32
SWAP = [(0, 1), (1, 0)]


def params(room):
    return pltpu.CompilerParams(vmem_limit_bytes=room * MIB)


def cost(flops, read):
    return pl.CostEstimate(flops=flops, bytes_accessed=read, transcendentals=0)


def hop(value, distance):
    total = lax.axis_size("tp")
    return lax.ppermute(value, "tp", [(i, i ^ distance) for i in range(total)])


def swap(value):
    return lax.ppermute(value, "fsdp", SWAP)


def contract_first(left, right):
    return lax.dot_general(left, right, (((0,), (0,)), ((), ())), preferred_element_type=F32)


VMEM = pl.BlockSpec(memory_space=pltpu.VMEM)
SMEM = pl.BlockSpec(memory_space=pltpu.SMEM)
ANY = pl.BlockSpec(memory_space=pl.ANY)


def in_vmem(value):
    return pltpu.with_memory_space_constraint(value, pltpu.VMEM)


def in_hbm(value):
    return pltpu.with_memory_space_constraint(value, pltpu.HBM)


def fetch_kernel(source, target, arrived):
    copy = pltpu.make_async_copy(source, target, arrived)
    copy.start()
    copy.wait()


def fetch(value, name):
    return pl.pallas_call(
        fetch_kernel,
        in_specs=[ANY],
        out_specs=VMEM,
        out_shape=pltpu.VMEM(value.shape, value.dtype),
        scratch_shapes=[pltpu.SemaphoreType.DMA],
        compiler_params=params(2),
        cost_estimate=cost(0, 2 * value.size),
        name=name,
    )(in_hbm(value))


def reach_kernel(lengths, values, bound, held, arrived):
    rows, slots, head_dim = values.shape
    copies = [
        pltpu.make_async_copy(values.at[row], held.at[row], arrived.at[row]) for row in range(rows)
    ]
    for copy in copies:
        copy.start()
    slot = lax.broadcasted_iota(jnp.int32, (slots, head_dim), 0)
    top = jnp.zeros((8, head_dim), F32)
    for row in range(rows):
        copies[row].wait()
        size = jnp.where(slot < lengths[row], jnp.abs(held[row].astype(F32)), 0.0)
        top = jnp.maximum(top, jnp.max(size.reshape(-1, 8, head_dim), axis=0))
    bound[...] = jnp.broadcast_to(jnp.max(top), bound.shape).astype(BF16)


def largest_in_reach(lengths, values, columns):
    return pl.pallas_call(
        reach_kernel,
        in_specs=[SMEM, ANY],
        out_specs=VMEM,
        out_shape=jax.ShapeDtypeStruct((16, columns), BF16),
        scratch_shapes=[
            pltpu.VMEM(values.shape, BF16),
            pltpu.SemaphoreType.DMA((values.shape[0],)),
        ],
        compiler_params=params(8),
        cost_estimate=cost(4 * values.size, 2 * values.size),
        name="largest_in_reach",
    )(lengths, in_hbm(values))


def query_kernel(
    place, near, far, upper, base, mine, theirs, effective, own, other, fresh, total, left
):
    outer, _, depth = near.shape
    rows = mine.shape[0]
    total[...] = jnp.zeros_like(total)

    def pair(z, _):
        for y, lower in ((0, near), (1, far)):
            start = pl.multiple_of(((2 * z + y) ^ place[0]) * depth, depth)
            block = pl.ds(start, depth)
            out = pltpu.make_async_copy(fresh.at[y], effective.at[block], left.at[y])

            @pl.when(z > 0)
            def _():
                out.wait()

            update = contract_first(lower[z], upper[...])
            fresh[y] = (base[block, :].astype(F32) + update).astype(BF16)
            out.start()
            both = jnp.concatenate([mine[:, block], theirs[:, block]], axis=0)
            total[...] += jnp.dot(both, fresh[y], preferred_element_type=F32)
        return 0

    lax.fori_loop(0, outer, pair, 0)
    own[...] = total[:rows]
    other[...] = total[rows:]
    for y in range(2):
        pltpu.make_async_copy(fresh.at[y], effective.at[pl.ds(0, depth)], left.at[y]).wait()


def query_project(place, near, far, upper, base, mine, theirs):
    depth = near.shape[2]
    width = base.shape[1]
    rows = mine.shape[0]
    return pl.pallas_call(
        query_kernel,
        in_specs=[SMEM] + [VMEM] * 6,
        out_specs=[ANY, VMEM, VMEM],
        out_shape=[
            jax.ShapeDtypeStruct(base.shape, BF16),
            jax.ShapeDtypeStruct((rows, width), F32),
            jax.ShapeDtypeStruct((rows, width), F32),
        ],
        scratch_shapes=[
            pltpu.VMEM((2, depth, width), BF16),
            pltpu.VMEM((2 * rows, width), F32),
            pltpu.SemaphoreType.DMA((2,)),
        ],
        compiler_params=params(14),
        cost_estimate=cost(2 * base.size * (near.shape[1] + 2 * rows), 2 * base.size),
        name="query_project",
    )(place, near, far, upper, in_vmem(base), mine, theirs)


def attend_kernel(
    steps, scale, lengths, own, other, bias, cosine, sine, keys, values, context,
    keys_held, values_held, arrived
):
    rows, slots, head_dim = keys.shape
    heads = own.shape[1] // head_dim
    group = 2
    copies = []
    for row in range(rows):
        copies.append(
            [
                pltpu.make_async_copy(keys.at[row], keys_held.at[row], arrived.at[0, row]),
                pltpu.make_async_copy(values.at[row], values_held.at[row], arrived.at[1, row]),
            ]
        )
        for copy in copies[row]:
            copy.start()
    slot = lax.broadcasted_iota(jnp.int32, (heads * steps, slots), 1)
    step = lax.broadcasted_iota(jnp.int32, (heads * steps, slots), 0) % steps
    behind = slot - step
    for first in range(0, rows, group):
        span = slice(first * steps, (first + group) * steps)
        query = (own[span] + other[span]) * scale + bias[...].astype(F32)
        turned = []
        for head in range(heads):
            part = query[:, head * head_dim : (head + 1) * head_dim]
            part = part * cosine[span] + pltpu.roll(part, head_dim // 2, 1) * sine[span]
            turned.append(part * head_dim ** (-0.5))
        gathered = []
        for row in range(group):
            for copy in copies[first + row]:
                copy.wait()
            queries = jnp.concatenate(
                [q[row * steps : (row + 1) * steps] for q in turned], axis=0
            ).astype(BF16)
            scores = lax.dot_general(
                queries,
                keys_held[first + row],
                (((1,), (1,)), ((), ())),
                preferred_element_type=F32,
            )
            scores = jnp.where(behind <= lengths[first + row] - steps, scores, F32(-1e30))
            top = jnp.max(scores, axis=-1, keepdims=True)
            weights = jnp.exp(scores - top)
            probs = (weights / jnp.sum(weights, axis=-1, keepdims=True)).astype(BF16)
            gathered.append(
                jnp.dot(probs, values_held[first + row], preferred_element_type=F32)
            )
        for head in range(heads):
            context[span, head * head_dim : (head + 1) * head_dim] = jnp.concatenate(
                [g[head * steps : (head + 1) * steps] for g in gathered], axis=0
            ).astype(BF16)


def attend(lengths, own, other, bias, cosine, sine, keys, values, steps, scale):
    rows = keys.shape[0]
    width = own.shape[1]
    return pl.pallas_call(
        functools.partial(attend_kernel, steps, scale),
        in_specs=[SMEM] + [VMEM] * 5 + [ANY] * 2,
        out_specs=VMEM,
        out_shape=jax.ShapeDtypeStruct((rows * steps, width), BF16),
        scratch_shapes=[
            pltpu.VMEM(keys.shape, BF16),
            pltpu.VMEM(values.shape, BF16),
            pltpu.SemaphoreType.DMA((2, rows)),
        ],
        compiler_params=params(18),
        cost_estimate=cost(4 * keys.size * width // keys.shape[2] * steps, 4 * keys.size),
        name="attend",
    )(lengths, own, other, bias, cosine, sine, in_hbm(keys), in_hbm(values))


def output_kernel(
    place, lower, upper, base, mine, theirs, effective, own, other, held, fresh, arrived, left
):
    outer = upper.shape[0]
    rank = lower.shape[0]
    width = upper.shape[3]
    rows = mine.shape[0]

    def columns(k):
        return pl.ds(pl.multiple_of((k ^ place[0]) * width, width), width)

    def fetch(k):
        return pltpu.make_async_copy(base.at[:, columns(k)], held.at[k], arrived.at[k])

    def ask(k, _):
        fetch(k).start()
        return 0

    lax.fori_loop(0, 2 * outer, ask, 0)
    both = jnp.concatenate([mine[...], theirs[...]], axis=0)

    def pair(z, _):
        for y in range(2):
            k = 2 * z + y
            out = pltpu.make_async_copy(fresh.at[y], effective.at[:, columns(k)], left.at[y])

            @pl.when(z > 0)
            def _():
                out.wait()

            update = contract_first(lower[...], upper[z, y, :rank])
            fetch(k).wait()
            fresh[y] = (held[k].astype(F32) + update).astype(BF16)
            out.start()
            product = jnp.dot(both, fresh[y], preferred_element_type=F32)
            own[y, z] = product[:rows]
            other[z, y] = product[rows:]
        return 0

    lax.fori_loop(0, outer, pair, 0)
    for y in range(2):
        pltpu.make_async_copy(fresh.at[y], effective.at[:, pl.ds(0, width)], left.at[y]).wait()


def output_project(place, lower, upper, base, mine, theirs):
    outer = upper.shape[0]
    width = upper.shape[3]
    depth = base.shape[0]
    rows = mine.shape[0]
    return pl.pallas_call(
        output_kernel,
        in_specs=[SMEM, VMEM, VMEM, ANY, VMEM, VMEM],
        out_specs=[ANY, VMEM, VMEM],
        out_shape=[
            jax.ShapeDtypeStruct(base.shape, BF16),
            jax.ShapeDtypeStruct((2, outer, rows, width), F32),
            jax.ShapeDtypeStruct((outer, 2, rows, width), F32),
        ],
        scratch_shapes=[
            pltpu.VMEM((2 * outer, depth, width), BF16),
            pltpu.VMEM((2, depth, width), BF16),
            pltpu.SemaphoreType.DMA((2 * outer,)),
            pltpu.SemaphoreType.DMA((2,)),
        ],
        compiler_params=params(24),
        cost_estimate=cost(2 * base.size * (lower.shape[0] + 2 * rows), 4 * base.size),
        name="output_project",
    )(place, lower, upper, in_hbm(base), mine, theirs)


def finish_kernel(place, bound, hidden, gain, near, far, residual, normed, combined):
    blocks, rows, width = near.shape
    half = blocks * width
    squares = jnp.zeros((rows, 1), F32)
    for pieces, which in ((near, place[1]), (far, 1 - place[1])):
        for k in range(blocks):
            start = pl.multiple_of(which * half + (place[0] ^ k) * width, width)
            total = hidden[:, pl.ds(start, width)].astype(F32) + pieces[k] * bound[0]
            combined[:, pl.ds(start, width)] = total
            residual[:, pl.ds(start, width)] = total.astype(BF16)
            squares += jnp.sum(total * total, axis=-1, keepdims=True)
    inverse = lax.rsqrt(squares / (2 * half) + NORM_EPS)
    normed[...] = (combined[...] * inverse * gain[...].astype(F32)).astype(BF16)


def finish(place, bound, hidden, gain, near, far):
    rows, whole = hidden.shape
    blocks, _, width = near.shape
    tall = 16
    spec = pltpu.PrefetchScalarGridSpec(
        num_scalar_prefetch=2,
        grid=(rows // tall,),
        in_specs=[
            pl.BlockSpec((tall, whole), lambda r, p, b: (r, 0)),
            pl.BlockSpec((1, whole), lambda r, p, b: (0, 0)),
            pl.BlockSpec((blocks, tall, width), lambda r, p, b: (0, r, 0)),
            pl.BlockSpec((blocks, tall, width), lambda r, p, b: (0, r, 0)),
        ],
        out_specs=[
            pl.BlockSpec((tall, whole), lambda r, p, b: (r, 0)),
            pl.BlockSpec((tall, whole), lambda r, p, b: (r, 0)),
        ],
        scratch_shapes=[pltpu.VMEM((tall, whole), F32)],
    )
    return pl.pallas_call(
        finish_kernel,
        grid_spec=spec,
        out_shape=[jax.ShapeDtypeStruct((rows, whole), BF16)] * 2,
        compiler_params=params(14),
        cost_estimate=cost(8 * hidden.size, 14 * hidden.size),
        name="finish",
    )(place, bound, hidden, gain, near, far)


def cross(value):
    total = lax.axis_size("tp")
    pairs = [(f * total + i, (1 - f) * total + (i ^ 1)) for f in range(2) for i in range(total)]
    return lax.ppermute(value, ("fsdp", "tp"), pairs)


def along_z(value):
    outer = lax.axis_size("tp") // 2
    return jnp.stack([value] + [hop(value, 2 * k) for k in range(1, outer)])


def along_y(value):
    return jnp.stack([value, hop(value, 1)])


def reduce_blocks(own, other, shrink):
    outer = other.shape[0]

    def narrow(value):
        return value.astype(F16)

    across = hop(narrow(shrink(own[1])), 1)
    arrived = [hop(narrow(shrink(other[k])), 2 * k) for k in range(1, outer)]
    summed = shrink(own[0]) + across.astype(F32)
    ended = [hop(narrow(summed[k]), 2 * k) for k in range(1, outer)]
    arrived, ended[:1] = lax.optimization_barrier((arrived, ended[:1]))
    total = summed[0] + sum(e.astype(F32) for e in ended)
    pair = narrow(shrink(other[0]) + sum(a.astype(F32) for a in arrived))
    far = swap(pair).astype(F32) + cross(pair)[::-1].astype(F32)
    return narrow(total), narrow(far)


def local(
    hidden_in,
    input_gain,
    post_gain,
    query_base_weight,
    query_bias,
    output_base_weight,
    query_lower_factor,
    query_upper_factor,
    output_lower_factor,
    output_upper_factor,
    cache_keys,
    cache_values,
    cache_lengths,
):
    rows, steps, width = hidden_in.shape
    tall = rows * steps
    half = width // 2
    slots, head_dim = cache_keys.shape[2:]
    features = query_base_weight.shape[1] * lax.axis_size("tp")
    t = lax.axis_index("tp").astype(jnp.int32)
    f = lax.axis_index("fsdp").astype(jnp.int32)
    place = jnp.stack([t, f])
    outer = lax.axis_size("tp") // 2

    lower_near = along_z(query_lower_factor.T)
    lower_far = hop(lower_near, 1)

    flat = hidden_in.reshape(tall, width)
    inputs32 = flat.astype(F32)
    mean_square = jnp.mean(inputs32 * inputs32, axis=-1, keepdims=True)
    normed = (inputs32 * lax.rsqrt(mean_square + NORM_EPS) * input_gain.astype(F32)).astype(BF16)
    mine = lax.dynamic_slice_in_dim(normed, f * half, half, 1)
    theirs = swap(lax.dynamic_slice_in_dim(normed, (1 - f) * half, half, 1))

    columns = query_upper_factor.shape[1]
    bound = largest_in_reach(cache_lengths, cache_values[:, 0], columns)
    rank_part = query_upper_factor.shape[0]
    sent = jnp.concatenate([query_upper_factor, output_lower_factor.T, bound], axis=0)
    came = swap(sent)

    def in_order(a, b):
        return jnp.where(f == 0, jnp.concatenate([a, b]), jnp.concatenate([b, a]))

    upper = in_order(sent[:rank_part], came[:rank_part]) * BF16(ADAPTER_SCALE)
    lower_o = in_order(sent[rank_part : 2 * rank_part], came[rank_part : 2 * rank_part])
    lower_o = lower_o * BF16(ADAPTER_SCALE)
    bound = jnp.maximum(sent[2 * rank_part :], came[2 * rank_part :])

    rank, block = output_upper_factor.shape
    message = jnp.concatenate([output_upper_factor, bound[:, :block]], axis=0)
    upper_o = along_z(along_y(message))
    bound = jnp.max(upper_o[:, :, rank:]).astype(F32)

    weight_q, _ = lax.optimization_barrier((query_base_weight, lower_near))
    query_effective, own, other = query_project(
        t[None], lower_near, lower_far, upper, fetch(weight_q, "fetch_query"), mine, theirs
    )
    other = swap(other)

    inverse = ROPE_BASE ** (-(np.arange(head_dim // 2) * 2.0) / head_dim)
    inverse = jnp.asarray(inverse.astype(np.float32))
    positions = cache_lengths[:, None] - steps + jnp.arange(steps, dtype=jnp.int32)[None, :]
    angles = positions.astype(F32).reshape(tall, 1) * inverse
    cosine, sine = jnp.cos(angles), jnp.sin(angles)
    context = attend(
        cache_lengths,
        own,
        other,
        query_bias[None, :],
        jnp.concatenate([cosine, cosine], axis=1),
        jnp.concatenate([-sine, sine], axis=1),
        cache_keys[:, 0],
        cache_values[:, 0],
        steps,
        width ** (-0.5),
    )

    output_effective, own, other = output_project(
        t[None], lower_o, upper_o, output_base_weight, context, swap(context)
    )

    small = 2.0**-16
    unit = jnp.maximum(bound, 1e-30) * small
    shrink_by = 1.0 / unit

    def shrink(value):
        return (value * shrink_by) * (features ** (-0.5) * small)

    near, far = reduce_blocks(own, other, shrink)

    near = along_z(near)
    near = jnp.stack([near, hop(near, 1)], axis=1)
    far = along_z(far)
    near = near.reshape((2 * outer,) + near.shape[2:]).astype(F32)
    far = far.reshape((2 * outer,) + far.shape[2:]).astype(F32)

    residual, normed_out = finish(
        place, jnp.maximum(bound, 1e-30)[None], flat, post_gain[None, :], near, far
    )
    return (
        residual.reshape(hidden_in.shape),
        normed_out.reshape(hidden_in.shape),
        query_effective,
        output_effective,
    )


def solution(mesh):
    in_specs = (
        P(("groups", "fsdp"), None, None),
        P(),
        P(),
        P("fsdp", "tp"),
        P("tp"),
        P("tp", "fsdp"),
        P(("fsdp", "tp"), None),
        P("fsdp", "tp"),
        P("tp", "fsdp"),
        P(None, ("fsdp", "tp")),
        P(("groups", "fsdp"), "tp", None, None),
        P(("groups", "fsdp"), "tp", None, None),
        P(("groups", "fsdp")),
    )
    out_specs = (
        P(("groups", "fsdp"), None, None),
        P(("groups", "fsdp"), None, None),
        P(("groups", "fsdp"), "tp"),
        P(("groups", "tp"), "fsdp"),
    )
    return jax.shard_map(local, mesh=mesh, in_specs=in_specs, out_specs=out_specs, check_vma=False)
```

```python
import functools

import jax
import jax.numpy as jnp
import numpy as np
from jax import lax
from jax.experimental import pallas as pl
from jax.experimental.pallas import tpu as pltpu
from jax.sharding import PartitionSpec as P

NORM_EPS = 1e-06
ROPE_BASE = 1000000.0
ADAPTER_SCALE = 0.5
MIB = 1024 * 1024
BF16 = jnp.bfloat16
F16 = jnp.float16
F32 = jnp.float32
SWAP = [(0, 1), (1, 0)]


def params(room):
    return pltpu.CompilerParams(vmem_limit_bytes=room * MIB)


def cost(flops, read):
    return pl.CostEstimate(flops=flops, bytes_accessed=read, transcendentals=0)


def hop(value, distance):
    total = lax.axis_size("tp")
    return lax.ppermute(value, "tp", [(i, i ^ distance) for i in range(total)])


def swap(value):
    return lax.ppermute(value, "fsdp", SWAP)


def contract_first(left, right):
    return lax.dot_general(left, right, (((0,), (0,)), ((), ())), preferred_element_type=F32)


VMEM = pl.BlockSpec(memory_space=pltpu.VMEM)
SMEM = pl.BlockSpec(memory_space=pltpu.SMEM)
ANY = pl.BlockSpec(memory_space=pl.ANY)


def in_vmem(value):
    return pltpu.with_memory_space_constraint(value, pltpu.VMEM)


def in_hbm(value):
    return pltpu.with_memory_space_constraint(value, pltpu.HBM)


def fetch_kernel(source, target, arrived):
    copy = pltpu.make_async_copy(source, target, arrived)
    copy.start()
    copy.wait()


def fetch(value, name):
    return pl.pallas_call(
        fetch_kernel,
        in_specs=[ANY],
        out_specs=VMEM,
        out_shape=pltpu.VMEM(value.shape, value.dtype),
        scratch_shapes=[pltpu.SemaphoreType.DMA],
        compiler_params=params(2),
        cost_estimate=cost(0, 2 * value.size),
        name=name,
    )(in_hbm(value))


def reach_kernel(lengths, values, upper, message, held, arrived, factor, factor_arrived):
    rows, slots, head_dim = values.shape
    rank, width = upper.shape
    copies = [
        pltpu.make_async_copy(values.at[row], held.at[row], arrived.at[row]) for row in range(rows)
    ]
    columns = pltpu.make_async_copy(upper, factor, factor_arrived)
    columns.start()
    for copy in copies:
        copy.start()
    slot = lax.broadcasted_iota(jnp.int32, (slots, head_dim), 0)
    top = jnp.zeros((8, head_dim), F32)
    for row in range(rows):
        copies[row].wait()
        size = jnp.where(slot < lengths[row], jnp.abs(held[row].astype(F32)), 0.0)
        top = jnp.maximum(top, jnp.max(size.reshape(-1, 8, head_dim), axis=0))
    columns.wait()
    for first in range(0, width, 128):
        message[first // 128 * rank : (first // 128 + 1) * rank] = factor[:, first : first + 128]
    message[width // 128 * rank :] = jnp.broadcast_to(jnp.max(top), (16, 128)).astype(BF16)


def with_largest_in_reach(lengths, values, upper):
    rank, width = upper.shape
    return pl.pallas_call(
        reach_kernel,
        in_specs=[SMEM, ANY, ANY],
        out_specs=VMEM,
        out_shape=jax.ShapeDtypeStruct((width // 128 * rank + 16, 128), BF16),
        scratch_shapes=[
            pltpu.VMEM(values.shape, BF16),
            pltpu.SemaphoreType.DMA((values.shape[0],)),
            pltpu.VMEM(upper.shape, BF16),
            pltpu.SemaphoreType.DMA,
        ],
        compiler_params=params(8),
        cost_estimate=cost(4 * values.size, 2 * values.size),
        name="with_largest_in_reach",
    )(lengths, in_hbm(values), in_hbm(upper))


def query_kernel(
    place, near, far, upper, base, mine, theirs, effective, own, other, fresh, total, left
):
    outer, _, depth = near.shape
    rows = mine.shape[0]
    total[...] = jnp.zeros_like(total)

    def pair(z, _):
        for y, lower in ((0, near), (1, far)):
            start = pl.multiple_of(((2 * z + y) ^ place[0]) * depth, depth)
            block = pl.ds(start, depth)
            out = pltpu.make_async_copy(fresh.at[y], effective.at[block], left.at[y])

            @pl.when(z > 0)
            def _():
                out.wait()

            update = contract_first(lower[z], upper[...])
            fresh[y] = (base[block, :].astype(F32) + update).astype(BF16)
            out.start()
            both = jnp.concatenate([mine[:, block], theirs[:, block]], axis=0)
            total[...] += jnp.dot(both, fresh[y], preferred_element_type=F32)
        return 0

    lax.fori_loop(0, outer, pair, 0)
    own[...] = total[:rows]
    other[...] = total[rows:]
    for y in range(2):
        pltpu.make_async_copy(fresh.at[y], effective.at[pl.ds(0, depth)], left.at[y]).wait()


def query_project(place, near, far, upper, base, mine, theirs):
    depth = near.shape[2]
    width = base.shape[1]
    rows = mine.shape[0]
    return pl.pallas_call(
        query_kernel,
        in_specs=[SMEM] + [VMEM] * 6,
        out_specs=[ANY, VMEM, VMEM],
        out_shape=[
            jax.ShapeDtypeStruct(base.shape, BF16),
            jax.ShapeDtypeStruct((rows, width), F32),
            jax.ShapeDtypeStruct((rows, width), F32),
        ],
        scratch_shapes=[
            pltpu.VMEM((2, depth, width), BF16),
            pltpu.VMEM((2 * rows, width), F32),
            pltpu.SemaphoreType.DMA((2,)),
        ],
        compiler_params=params(14),
        cost_estimate=cost(2 * base.size * (near.shape[1] + 2 * rows), 2 * base.size),
        name="query_project",
    )(place, near, far, upper, in_vmem(base), mine, theirs)


def attend_kernel(
    steps, scale, lengths, own, other, bias, cosine, sine, keys, values, context,
    keys_held, values_held, arrived
):
    rows, slots, head_dim = keys.shape
    heads = own.shape[1] // head_dim
    copies = []
    for row in range(rows):
        copies.append(
            [
                pltpu.make_async_copy(keys.at[row], keys_held.at[row], arrived.at[0, row]),
                pltpu.make_async_copy(values.at[row], values_held.at[row], arrived.at[1, row]),
            ]
        )
        for copy in copies[row]:
            copy.start()
    slot = lax.broadcasted_iota(jnp.int32, (heads * steps, slots), 1)
    step = lax.broadcasted_iota(jnp.int32, (heads * steps, slots), 0) % steps
    behind = slot - step
    many = heads * steps
    nothing = jnp.zeros((many, head_dim), F32)
    for first in range(0, rows, 2):
        pair = (first, first + 1)
        span = slice(first * steps, (first + 2) * steps)
        query = (own[span] + other[span]) * scale + bias[...].astype(F32)
        turned = []
        for head in range(heads):
            part = query[:, head * head_dim : (head + 1) * head_dim]
            part = part * cosine[span] + pltpu.roll(part, head_dim // 2, 1) * sine[span]
            turned.append(part * head_dim ** (-0.5))
        upper, lower = [
            jnp.concatenate([q[i * steps : (i + 1) * steps] for q in turned], axis=0) for i in (0, 1)
        ]
        queries = jnp.concatenate(
            [
                jnp.concatenate([upper, nothing], axis=1),
                jnp.concatenate([nothing, lower], axis=1),
            ],
            axis=0,
        ).astype(BF16)
        for row in pair:
            copies[row][0].wait()
        both = jnp.concatenate([keys_held[row] for row in pair], axis=1)
        scores = lax.dot_general(
            queries, both, (((1,), (1,)), ((), ())), preferred_element_type=F32
        )
        scores = jnp.concatenate(
            [
                jnp.where(
                    behind <= lengths[first + i] - steps,
                    scores[i * many : (i + 1) * many],
                    F32(-1e30),
                )
                for i in (0, 1)
            ],
            axis=0,
        )
        top = jnp.max(scores, axis=-1, keepdims=True)
        weights = jnp.exp(scores - top)
        probs = (weights / jnp.sum(weights, axis=-1, keepdims=True)).astype(BF16)
        for row in pair:
            copies[row][1].wait()
        both = jnp.concatenate([values_held[row] for row in pair], axis=1)
        mixed = jnp.dot(probs, both, preferred_element_type=F32)
        gathered = (mixed[:many, :head_dim], mixed[many:, head_dim:])
        for head in range(heads):
            context[span, head * head_dim : (head + 1) * head_dim] = jnp.concatenate(
                [g[head * steps : (head + 1) * steps] for g in gathered], axis=0
            ).astype(BF16)


def attend(lengths, own, other, bias, cosine, sine, keys, values, steps, scale):
    rows = keys.shape[0]
    width = own.shape[1]
    return pl.pallas_call(
        functools.partial(attend_kernel, steps, scale),
        in_specs=[SMEM] + [VMEM] * 5 + [ANY] * 2,
        out_specs=VMEM,
        out_shape=jax.ShapeDtypeStruct((rows * steps, width), BF16),
        scratch_shapes=[
            pltpu.VMEM(keys.shape, BF16),
            pltpu.VMEM(values.shape, BF16),
            pltpu.SemaphoreType.DMA((2, rows)),
        ],
        compiler_params=params(18),
        cost_estimate=cost(4 * keys.size * width // keys.shape[2] * steps, 4 * keys.size),
        name="attend",
    )(lengths, own, other, bias, cosine, sine, in_hbm(keys), in_hbm(values))


def output_kernel(
    place, lower, upper, base, mine, theirs, effective, own, other, held, fresh, arrived, left
):
    outer = upper.shape[0]
    rank = lower.shape[0]
    width = fresh.shape[2]
    rows = mine.shape[0]

    def columns(k):
        return pl.ds(pl.multiple_of((k ^ place[0]) * width, width), width)

    def fetch(k):
        return pltpu.make_async_copy(base.at[:, columns(k)], held.at[k], arrived.at[k])

    def ask(k, _):
        fetch(k).start()
        return 0

    lax.fori_loop(0, 2 * outer, ask, 0)
    both = jnp.concatenate([mine[...], theirs[...]], axis=0)

    def pair(z, _):
        for y in range(2):
            k = 2 * z + y
            out = pltpu.make_async_copy(fresh.at[y], effective.at[:, columns(k)], left.at[y])

            @pl.when(z > 0)
            def _():
                out.wait()

            factor = [upper[z, y, n * rank : (n + 1) * rank] for n in range(width // 128)]
            update = contract_first(lower[...], jnp.concatenate(factor, axis=1))
            fetch(k).wait()
            fresh[y] = (held[k].astype(F32) + update).astype(BF16)
            out.start()
            product = jnp.dot(both, fresh[y], preferred_element_type=F32)
            own[y, z] = product[:rows]
            other[z, y] = product[rows:]
        return 0

    lax.fori_loop(0, outer, pair, 0)
    for y in range(2):
        pltpu.make_async_copy(fresh.at[y], effective.at[:, pl.ds(0, width)], left.at[y]).wait()


def output_project(place, lower, upper, base, mine, theirs):
    outer = upper.shape[0]
    width = base.shape[1] // (2 * outer)
    depth = base.shape[0]
    rows = mine.shape[0]
    return pl.pallas_call(
        output_kernel,
        in_specs=[SMEM, VMEM, VMEM, ANY, VMEM, VMEM],
        out_specs=[ANY, VMEM, VMEM],
        out_shape=[
            jax.ShapeDtypeStruct(base.shape, BF16),
            jax.ShapeDtypeStruct((2, outer, rows, width), F32),
            jax.ShapeDtypeStruct((outer, 2, rows, width), F32),
        ],
        scratch_shapes=[
            pltpu.VMEM((2 * outer, depth, width), BF16),
            pltpu.VMEM((2, depth, width), BF16),
            pltpu.SemaphoreType.DMA((2 * outer,)),
            pltpu.SemaphoreType.DMA((2,)),
        ],
        compiler_params=params(24),
        cost_estimate=cost(2 * base.size * (lower.shape[0] + 2 * rows), 4 * base.size),
        name="output_project",
    )(place, lower, upper, in_hbm(base), mine, theirs)


def finish_kernel(place, bound, hidden, gain, near, far, residual, normed, combined, held, left):
    blocks, rows, width = near.shape
    half = blocks * width
    tall = combined.shape[0]

    def put(which, out, first):
        slot = first // tall % 2
        return pltpu.make_async_copy(
            held.at[which, slot], out.at[pl.ds(first, tall)], left.at[which, slot]
        )

    for first in range(0, rows, tall):
        slot = first // tall % 2
        if first >= 2 * tall:
            put(0, residual, first - 2 * tall).wait()
            put(1, normed, first - 2 * tall).wait()
        squares = jnp.zeros((tall, 128), F32)
        for pieces, which in ((near, place[1]), (far, 1 - place[1])):
            for k in range(blocks):
                start = pl.multiple_of(which * half + (place[0] ^ k) * width, width)
                total = hidden[first : first + tall, pl.ds(start, width)].astype(F32)
                total += pieces[k, first : first + tall] * bound[0]
                combined[:, pl.ds(start, width)] = total
                held[0, slot, :, pl.ds(start, width)] = total.astype(BF16)
                for lane in range(0, width, 128):
                    squares += total[:, lane : lane + 128] * total[:, lane : lane + 128]
        put(0, residual, first).start()
        mean = jnp.sum(squares, axis=-1, keepdims=True) / (2 * half)
        inverse = lax.rsqrt(mean + NORM_EPS)
        held[1, slot] = (combined[...] * inverse * gain[...].astype(F32)).astype(BF16)
        put(1, normed, first).start()
    for first in range(max(rows - 2 * tall, 0), rows, tall):
        put(0, residual, first).wait()
        put(1, normed, first).wait()


def finish(place, bound, hidden, gain, near, far):
    rows, whole = hidden.shape
    tall = 16
    return pl.pallas_call(
        finish_kernel,
        in_specs=[SMEM, SMEM] + [VMEM] * 4,
        out_specs=[ANY, ANY],
        out_shape=[jax.ShapeDtypeStruct((rows, whole), BF16)] * 2,
        scratch_shapes=[
            pltpu.VMEM((tall, whole), F32),
            pltpu.VMEM((2, 2, tall, whole), BF16),
            pltpu.SemaphoreType.DMA((2, 2)),
        ],
        compiler_params=params(14),
        cost_estimate=cost(8 * hidden.size, 14 * hidden.size),
        name="finish",
    )(place, bound, hidden, gain, near, far)


def cross(value):
    total = lax.axis_size("tp")
    pairs = [(f * total + i, (1 - f) * total + (i ^ 1)) for f in range(2) for i in range(total)]
    return lax.ppermute(value, ("fsdp", "tp"), pairs)


def along_z(value):
    outer = lax.axis_size("tp") // 2
    return jnp.stack([value] + [hop(value, 2 * k) for k in range(1, outer)])


def along_y(value):
    return jnp.stack([value, hop(value, 1)])


def reduce_blocks(own, other, shrink):
    outer = other.shape[0]

    def narrow(value):
        return value.astype(F16)

    across = hop(narrow(shrink(own[1])), 1)
    arrived = [hop(narrow(shrink(other[k])), 2 * k) for k in range(1, outer)]
    summed = shrink(own[0]) + across.astype(F32)
    ended = [hop(narrow(summed[k]), 2 * k) for k in range(1, outer)]
    arrived, ended[:1] = lax.optimization_barrier((arrived, ended[:1]))
    total = summed[0] + sum(e.astype(F32) for e in ended)
    pair = narrow(shrink(other[0]) + sum(a.astype(F32) for a in arrived))
    far = swap(pair).astype(F32) + cross(pair)[::-1].astype(F32)
    return narrow(total), narrow(far)


def local(
    hidden_in,
    input_gain,
    post_gain,
    query_base_weight,
    query_bias,
    output_base_weight,
    query_lower_factor,
    query_upper_factor,
    output_lower_factor,
    output_upper_factor,
    cache_keys,
    cache_values,
    cache_lengths,
):
    rows, steps, width = hidden_in.shape
    tall = rows * steps
    half = width // 2
    slots, head_dim = cache_keys.shape[2:]
    features = query_base_weight.shape[1] * lax.axis_size("tp")
    t = lax.axis_index("tp").astype(jnp.int32)
    f = lax.axis_index("fsdp").astype(jnp.int32)
    place = jnp.stack([t, f])
    outer = lax.axis_size("tp") // 2

    lower_near = along_z(query_lower_factor.T)
    lower_far = hop(lower_near, 1)

    rank_part = query_upper_factor.shape[0]
    sent = jnp.concatenate([query_upper_factor, output_lower_factor.T], axis=0)
    came = swap(sent)

    def in_order(a, b):
        return jnp.where(f == 0, jnp.concatenate([a, b]), jnp.concatenate([b, a]))

    upper = in_order(sent[:rank_part], came[:rank_part]) * BF16(ADAPTER_SCALE)
    lower_o = in_order(sent[rank_part:], came[rank_part:]) * BF16(ADAPTER_SCALE)

    message = with_largest_in_reach(cache_lengths, cache_values[:, 0], output_upper_factor)
    bound = jnp.maximum(message[-16:], swap(message[-16:]))

    hidden, message = lax.optimization_barrier((hidden_in, message))
    flat = hidden.reshape(tall, width)
    inputs32 = flat.astype(F32)
    mean_square = jnp.mean(inputs32 * inputs32, axis=-1, keepdims=True)
    normed = (inputs32 * lax.rsqrt(mean_square + NORM_EPS) * input_gain.astype(F32)).astype(BF16)
    mine = lax.dynamic_slice_in_dim(normed, f * half, half, 1)
    theirs = swap(lax.dynamic_slice_in_dim(normed, (1 - f) * half, half, 1))

    message = jnp.concatenate([message[:-16], bound], axis=0)
    message, lower_near = lax.optimization_barrier((message, lower_near))
    upper_o = along_z(along_y(message))
    bound = jnp.max(upper_o[:, :, -16:]).astype(F32)

    weight_q, _ = lax.optimization_barrier((query_base_weight, lower_near))
    query_effective, own, other = query_project(
        t[None], lower_near, lower_far, upper, fetch(weight_q, "fetch_query"), mine, theirs
    )
    other = swap(other)

    inverse = ROPE_BASE ** (-(np.arange(head_dim // 2) * 2.0) / head_dim)
    inverse = jnp.asarray(inverse.astype(np.float32))
    positions = cache_lengths[:, None] - steps + jnp.arange(steps, dtype=jnp.int32)[None, :]
    angles = positions.astype(F32).reshape(tall, 1) * inverse
    cosine, sine = jnp.cos(angles), jnp.sin(angles)
    context = attend(
        cache_lengths,
        own,
        other,
        query_bias[None, :],
        jnp.concatenate([cosine, cosine], axis=1),
        jnp.concatenate([-sine, sine], axis=1),
        cache_keys[:, 0],
        cache_values[:, 0],
        steps,
        width ** (-0.5),
    )

    output_effective, own, other = output_project(
        t[None], lower_o, upper_o, output_base_weight, context, swap(context)
    )

    small = 2.0**-16
    unit = jnp.maximum(bound, 1e-30) * small
    shrink_by = 1.0 / unit

    def shrink(value):
        return (value * shrink_by) * (features ** (-0.5) * small)

    near, far = reduce_blocks(own, other, shrink)

    near = along_z(near)
    near = jnp.stack([near, hop(near, 1)], axis=1)
    far = along_z(far)
    near = near.reshape((2 * outer,) + near.shape[2:]).astype(F32)
    far = far.reshape((2 * outer,) + far.shape[2:]).astype(F32)

    residual, normed_out = finish(
        place, jnp.maximum(bound, 1e-30)[None], flat, post_gain[None, :], near, far
    )
    return (
        residual.reshape(hidden_in.shape),
        normed_out.reshape(hidden_in.shape),
        query_effective,
        output_effective,
    )


def solution(mesh):
    in_specs = (
        P(("groups", "fsdp"), None, None),
        P(),
        P(),
        P("fsdp", "tp"),
        P("tp"),
        P("tp", "fsdp"),
        P(("fsdp", "tp"), None),
        P("fsdp", "tp"),
        P("tp", "fsdp"),
        P(None, ("fsdp", "tp")),
        P(("groups", "fsdp"), "tp", None, None),
        P(("groups", "fsdp"), "tp", None, None),
        P(("groups", "fsdp")),
    )
    out_specs = (
        P(("groups", "fsdp"), None, None),
        P(("groups", "fsdp"), None, None),
        P(("groups", "fsdp"), "tp"),
        P(("groups", "tp"), "fsdp"),
    )
    return jax.shard_map(local, mesh=mesh, in_specs=in_specs, out_specs=out_specs, check_vma=False)
```

```python
import functools

import jax
import jax.numpy as jnp
import numpy as np
from jax import lax
from jax.experimental import pallas as pl
from jax.experimental.pallas import tpu as pltpu
from jax.sharding import PartitionSpec as P

NORM_EPS = 1e-06
ROPE_BASE = 1000000.0
ADAPTER_SCALE = 0.5
MIB = 1024 * 1024
BF16 = jnp.bfloat16
F16 = jnp.float16
F32 = jnp.float32
SWAP = [(0, 1), (1, 0)]


def params(room):
    return pltpu.CompilerParams(vmem_limit_bytes=room * MIB)


def cost(flops, read):
    return pl.CostEstimate(flops=flops, bytes_accessed=read, transcendentals=0)


def hop(value, distance):
    total = lax.axis_size("tp")
    return lax.ppermute(value, "tp", [(i, i ^ distance) for i in range(total)])


def swap(value):
    return lax.ppermute(value, "fsdp", SWAP)


def contract_first(left, right):
    return lax.dot_general(left, right, (((0,), (0,)), ((), ())), preferred_element_type=F32)


VMEM = pl.BlockSpec(memory_space=pltpu.VMEM)
SMEM = pl.BlockSpec(memory_space=pltpu.SMEM)
ANY = pl.BlockSpec(memory_space=pl.ANY)


def in_vmem(value):
    return pltpu.with_memory_space_constraint(value, pltpu.VMEM)


def in_hbm(value):
    return pltpu.with_memory_space_constraint(value, pltpu.HBM)


def fetch_kernel(source, target, arrived):
    copy = pltpu.make_async_copy(source, target, arrived)
    copy.start()
    copy.wait()


def fetch(value, name):
    return pl.pallas_call(
        fetch_kernel,
        in_specs=[ANY],
        out_specs=VMEM,
        out_shape=pltpu.VMEM(value.shape, value.dtype),
        scratch_shapes=[pltpu.SemaphoreType.DMA],
        compiler_params=params(2),
        cost_estimate=cost(0, 2 * value.size),
        name=name,
    )(in_hbm(value))


def reach_kernel(lengths, values, upper, message, held, arrived, factor, factor_arrived):
    rows, slots, head_dim = values.shape
    rank, width = upper.shape
    copies = [
        pltpu.make_async_copy(values.at[row], held.at[row], arrived.at[row]) for row in range(rows)
    ]
    columns = pltpu.make_async_copy(upper, factor, factor_arrived)
    columns.start()
    for copy in copies:
        copy.start()
    part = 256
    slot = lax.broadcasted_iota(jnp.int32, (part, head_dim), 0)
    top = jnp.zeros((16, head_dim), BF16)
    edge = jnp.zeros((8, head_dim), F32)
    for row in range(rows):
        copies[row].wait()
        whole = lengths[row] // part

        def full(n, top, row=row):
            size = jnp.abs(held[row, pl.ds(pl.multiple_of(n * part, part), part)])
            return jnp.maximum(top, jnp.max(size.reshape(-1, 16, head_dim), axis=0))

        top = lax.fori_loop(0, whole, full, top)
        last = pl.multiple_of(jnp.minimum(whole, slots // part - 1) * part, part)
        size = jnp.abs(held[row, pl.ds(last, part)].astype(F32))
        size = jnp.where(slot < lengths[row] - last, size, 0.0)
        edge = jnp.maximum(edge, jnp.max(size.reshape(-1, 8, head_dim), axis=0))
    most = jnp.maximum(jnp.max(top.astype(F32)), jnp.max(edge))
    columns.wait()
    for first in range(0, width, 128):
        message[first // 128 * rank : (first // 128 + 1) * rank] = factor[:, first : first + 128]
    message[width // 128 * rank :] = jnp.broadcast_to(most, (16, 128)).astype(BF16)


def with_largest_in_reach(lengths, values, upper):
    rank, width = upper.shape
    return pl.pallas_call(
        reach_kernel,
        in_specs=[SMEM, ANY, ANY],
        out_specs=VMEM,
        out_shape=jax.ShapeDtypeStruct((width // 128 * rank + 16, 128), BF16),
        scratch_shapes=[
            pltpu.VMEM(values.shape, BF16),
            pltpu.SemaphoreType.DMA((values.shape[0],)),
            pltpu.VMEM(upper.shape, BF16),
            pltpu.SemaphoreType.DMA,
        ],
        compiler_params=params(8),
        cost_estimate=cost(4 * values.size, 2 * values.size),
        name="with_largest_in_reach",
    )(lengths, in_hbm(values), in_hbm(upper))


def query_kernel(y, place, lower, upper, base, mine, theirs, *refs):
    before, (effective, own, other, fresh, total, left) = refs[: 3 * y], refs[3 * y :]
    outer, _, depth = lower.shape
    rows = mine.shape[0]
    if y:
        total[:rows] = before[1][...]
        total[rows:] = before[2][...]
    else:
        total[...] = jnp.zeros_like(total)

    def pair(half, _):
        for slot in range(2):
            z = 2 * half + slot
            start = pl.multiple_of(((2 * z + y) ^ place[0]) * depth, depth)
            block = pl.ds(start, depth)
            out = pltpu.make_async_copy(fresh.at[slot], effective.at[block], left.at[slot])

            @pl.when(half > 0)
            def _():
                out.wait()

            update = contract_first(lower[z], upper[...])
            fresh[slot] = (base[block, :].astype(F32) + update).astype(BF16)
            out.start()
            both = jnp.concatenate([mine[:, block], theirs[:, block]], axis=0)
            total[...] += jnp.dot(both, fresh[slot], preferred_element_type=F32)
        return 0

    lax.fori_loop(0, outer // 2, pair, 0)
    own[...] = total[:rows]
    other[...] = total[rows:]
    for slot in range(2):
        pltpu.make_async_copy(
            fresh.at[slot], effective.at[pl.ds(0, depth)], left.at[slot]
        ).wait()


def query_project(y, place, lower, upper, base, mine, theirs, before=()):
    depth = lower.shape[2]
    width = base.shape[1]
    rows = mine.shape[0]
    return pl.pallas_call(
        functools.partial(query_kernel, y),
        in_specs=[SMEM] + [VMEM] * 5 + [ANY, VMEM, VMEM][: len(before)],
        out_specs=[ANY, VMEM, VMEM],
        out_shape=[
            jax.ShapeDtypeStruct(base.shape, BF16),
            jax.ShapeDtypeStruct((rows, width), F32),
            jax.ShapeDtypeStruct((rows, width), F32),
        ],
        scratch_shapes=[
            pltpu.VMEM((2, depth, width), BF16),
            pltpu.VMEM((2 * rows, width), F32),
            pltpu.SemaphoreType.DMA((2,)),
        ],
        input_output_aliases={6: 0} if before else {},
        compiler_params=params(14),
        cost_estimate=cost(base.size * (lower.shape[1] + 2 * rows), base.size),
        name="query_project",
    )(place, lower, upper, in_vmem(base), mine, theirs, *before)


def attend_kernel(
    steps, scale, lengths, own, other, bias, cosine, sine, keys, values, context,
    keys_held, values_held, arrived
):
    rows, slots, head_dim = keys.shape
    heads = own.shape[1] // head_dim
    copies = []
    for row in range(rows):
        copies.append(
            [
                pltpu.make_async_copy(keys.at[row], keys_held.at[row], arrived.at[0, row]),
                pltpu.make_async_copy(values.at[row], values_held.at[row], arrived.at[1, row]),
            ]
        )
        for copy in copies[row]:
            copy.start()
    slot = lax.broadcasted_iota(jnp.int32, (heads * steps, slots), 1)
    step = lax.broadcasted_iota(jnp.int32, (heads * steps, slots), 0) % steps
    behind = slot - step
    many = heads * steps
    nothing = jnp.zeros((many, head_dim), F32)
    for first in range(0, rows, 2):
        pair = (first, first + 1)
        span = slice(first * steps, (first + 2) * steps)
        query = (own[span] + other[span]) * scale + bias[...].astype(F32)
        turned = []
        for head in range(heads):
            part = query[:, head * head_dim : (head + 1) * head_dim]
            part = part * cosine[span] + pltpu.roll(part, head_dim // 2, 1) * sine[span]
            turned.append(part * head_dim ** (-0.5))
        upper, lower = [
            jnp.concatenate([q[i * steps : (i + 1) * steps] for q in turned], axis=0) for i in (0, 1)
        ]
        queries = jnp.concatenate(
            [
                jnp.concatenate([upper, nothing], axis=1),
                jnp.concatenate([nothing, lower], axis=1),
            ],
            axis=0,
        ).astype(BF16)
        for row in pair:
            copies[row][0].wait()
        both = jnp.concatenate([keys_held[row] for row in pair], axis=1)
        scores = lax.dot_general(
            queries, both, (((1,), (1,)), ((), ())), preferred_element_type=F32
        )
        scores = jnp.concatenate(
            [
                jnp.where(
                    behind <= lengths[first + i] - steps,
                    scores[i * many : (i + 1) * many],
                    F32(-1e30),
                )
                for i in (0, 1)
            ],
            axis=0,
        )
        top = jnp.max(scores, axis=-1, keepdims=True)
        weights = jnp.exp(scores - top)
        probs = (weights / jnp.sum(weights, axis=-1, keepdims=True)).astype(BF16)
        for row in pair:
            copies[row][1].wait()
        both = jnp.concatenate([values_held[row] for row in pair], axis=1)
        mixed = jnp.dot(probs, both, preferred_element_type=F32)
        gathered = (mixed[:many, :head_dim], mixed[many:, head_dim:])
        for head in range(heads):
            context[span, head * head_dim : (head + 1) * head_dim] = jnp.concatenate(
                [g[head * steps : (head + 1) * steps] for g in gathered], axis=0
            ).astype(BF16)


def attend(lengths, own, other, bias, cosine, sine, keys, values, steps, scale):
    rows = keys.shape[0]
    width = own.shape[1]
    return pl.pallas_call(
        functools.partial(attend_kernel, steps, scale),
        in_specs=[SMEM] + [VMEM] * 5 + [ANY] * 2,
        out_specs=VMEM,
        out_shape=jax.ShapeDtypeStruct((rows * steps, width), BF16),
        scratch_shapes=[
            pltpu.VMEM(keys.shape, BF16),
            pltpu.VMEM(values.shape, BF16),
            pltpu.SemaphoreType.DMA((2, rows)),
        ],
        compiler_params=params(18),
        cost_estimate=cost(4 * keys.size * width // keys.shape[2] * steps, 4 * keys.size),
        name="attend",
    )(lengths, own, other, bias, cosine, sine, in_hbm(keys), in_hbm(values))


def output_kernel(
    place, lower, upper, base, mine, theirs, effective, own, other, held, fresh, arrived, left
):
    outer = upper.shape[0]
    rank = lower.shape[0]
    width = fresh.shape[2]
    rows = mine.shape[0]

    def columns(k):
        return pl.ds(pl.multiple_of((k ^ place[0]) * width, width), width)

    def fetch(k):
        return pltpu.make_async_copy(base.at[:, columns(k)], held.at[k], arrived.at[k])

    def ask(k, _):
        fetch(k).start()
        return 0

    lax.fori_loop(0, 2 * outer, ask, 0)
    both = jnp.concatenate([mine[...], theirs[...]], axis=0)

    def pair(z, _):
        for y in range(2):
            k = 2 * z + y
            out = pltpu.make_async_copy(fresh.at[y], effective.at[:, columns(k)], left.at[y])

            @pl.when(z > 0)
            def _():
                out.wait()

            factor = [upper[z, y, n * rank : (n + 1) * rank] for n in range(width // 128)]
            update = contract_first(lower[...], jnp.concatenate(factor, axis=1))
            fetch(k).wait()
            fresh[y] = (held[k].astype(F32) + update).astype(BF16)
            out.start()
            product = jnp.dot(both, fresh[y], preferred_element_type=F32)
            own[y, z] = product[:rows]
            other[z, y] = product[rows:]
        return 0

    lax.fori_loop(0, outer, pair, 0)
    for y in range(2):
        pltpu.make_async_copy(fresh.at[y], effective.at[:, pl.ds(0, width)], left.at[y]).wait()


def output_project(place, lower, upper, base, mine, theirs):
    outer = upper.shape[0]
    width = base.shape[1] // (2 * outer)
    depth = base.shape[0]
    rows = mine.shape[0]
    return pl.pallas_call(
        output_kernel,
        in_specs=[SMEM, VMEM, VMEM, ANY, VMEM, VMEM],
        out_specs=[ANY, VMEM, VMEM],
        out_shape=[
            jax.ShapeDtypeStruct(base.shape, BF16),
            jax.ShapeDtypeStruct((2, outer, rows, width), F32),
            jax.ShapeDtypeStruct((outer, 2, rows, width), F32),
        ],
        scratch_shapes=[
            pltpu.VMEM((2 * outer, depth, width), BF16),
            pltpu.VMEM((2, depth, width), BF16),
            pltpu.SemaphoreType.DMA((2 * outer,)),
            pltpu.SemaphoreType.DMA((2,)),
        ],
        compiler_params=params(24),
        cost_estimate=cost(2 * base.size * (lower.shape[0] + 2 * rows), 4 * base.size),
        name="output_project",
    )(place, lower, upper, in_hbm(base), mine, theirs)


def finish_kernel(place, bound, hidden, gain, near, far, residual, normed, combined, held, left):
    blocks, rows, width = near.shape
    half = blocks * width
    tall = combined.shape[0]

    def put(which, out, first):
        slot = first // tall % 2
        return pltpu.make_async_copy(
            held.at[which, slot], out.at[pl.ds(first, tall)], left.at[which, slot]
        )

    for first in range(0, rows, tall):
        slot = first // tall % 2
        if first >= 2 * tall:
            put(0, residual, first - 2 * tall).wait()
            put(1, normed, first - 2 * tall).wait()
        squares = jnp.zeros((tall, 128), F32)
        for pieces, which in ((near, place[1]), (far, 1 - place[1])):
            for k in range(blocks):
                start = pl.multiple_of(which * half + (place[0] ^ k) * width, width)
                total = hidden[first : first + tall, pl.ds(start, width)].astype(F32)
                total += pieces[k, first : first + tall] * bound[0]
                combined[:, pl.ds(start, width)] = total
                held[0, slot, :, pl.ds(start, width)] = total.astype(BF16)
                for lane in range(0, width, 128):
                    squares += total[:, lane : lane + 128] * total[:, lane : lane + 128]
        put(0, residual, first).start()
        mean = jnp.sum(squares, axis=-1, keepdims=True) / (2 * half)
        inverse = lax.rsqrt(mean + NORM_EPS)
        held[1, slot] = (combined[...] * inverse * gain[...].astype(F32)).astype(BF16)
        put(1, normed, first).start()
    for first in range(max(rows - 2 * tall, 0), rows, tall):
        put(0, residual, first).wait()
        put(1, normed, first).wait()


def finish(place, bound, hidden, gain, near, far):
    rows, whole = hidden.shape
    tall = 16
    return pl.pallas_call(
        finish_kernel,
        in_specs=[SMEM, SMEM] + [VMEM] * 4,
        out_specs=[ANY, ANY],
        out_shape=[jax.ShapeDtypeStruct((rows, whole), BF16)] * 2,
        scratch_shapes=[
            pltpu.VMEM((tall, whole), F32),
            pltpu.VMEM((2, 2, tall, whole), BF16),
            pltpu.SemaphoreType.DMA((2, 2)),
        ],
        compiler_params=params(14),
        cost_estimate=cost(8 * hidden.size, 14 * hidden.size),
        name="finish",
    )(place, bound, hidden, gain, near, far)


def cross(value):
    total = lax.axis_size("tp")
    pairs = [(f * total + i, (1 - f) * total + (i ^ 1)) for f in range(2) for i in range(total)]
    return lax.ppermute(value, ("fsdp", "tp"), pairs)


def along_z(value):
    outer = lax.axis_size("tp") // 2
    return jnp.stack([value] + [hop(value, 2 * k) for k in range(1, outer)])


def along_y(value):
    return jnp.stack([value, hop(value, 1)])


def reduce_blocks(own, other, shrink):
    outer = other.shape[0]

    def narrow(value):
        return value.astype(F16)

    across = hop(narrow(shrink(own[1])), 1)
    arrived = [hop(narrow(shrink(other[k])), 2 * k) for k in range(1, outer)]
    summed = shrink(own[0]) + across.astype(F32)
    ended = [hop(narrow(summed[k]), 2 * k) for k in range(1, outer)]
    arrived, ended[:1] = lax.optimization_barrier((arrived, ended[:1]))
    total = summed[0] + sum(e.astype(F32) for e in ended)
    pair = narrow(shrink(other[0]) + sum(a.astype(F32) for a in arrived))
    far = swap(pair).astype(F32) + cross(pair)[::-1].astype(F32)
    return narrow(total), narrow(far)


def local(
    hidden_in,
    input_gain,
    post_gain,
    query_base_weight,
    query_bias,
    output_base_weight,
    query_lower_factor,
    query_upper_factor,
    output_lower_factor,
    output_upper_factor,
    cache_keys,
    cache_values,
    cache_lengths,
):
    rows, steps, width = hidden_in.shape
    tall = rows * steps
    half = width // 2
    slots, head_dim = cache_keys.shape[2:]
    features = query_base_weight.shape[1] * lax.axis_size("tp")
    t = lax.axis_index("tp").astype(jnp.int32)
    f = lax.axis_index("fsdp").astype(jnp.int32)
    place = jnp.stack([t, f])
    outer = lax.axis_size("tp") // 2

    lower_near = along_z(query_lower_factor.T)
    lower_far = hop(lower_near, 1)

    rank_part = query_upper_factor.shape[0]
    sent = jnp.concatenate([query_upper_factor, output_lower_factor.T], axis=0)
    came = swap(sent)

    def in_order(a, b):
        return jnp.where(f == 0, jnp.concatenate([a, b]), jnp.concatenate([b, a]))

    upper = in_order(sent[:rank_part], came[:rank_part]) * BF16(ADAPTER_SCALE)
    lower_o = in_order(sent[rank_part:], came[rank_part:]) * BF16(ADAPTER_SCALE)

    message = with_largest_in_reach(cache_lengths, cache_values[:, 0], output_upper_factor)
    bound = jnp.maximum(message[-16:], swap(message[-16:]))

    hidden, message = lax.optimization_barrier((hidden_in, message))
    flat = hidden.reshape(tall, width)
    inputs32 = flat.astype(F32)
    mean_square = jnp.mean(inputs32 * inputs32, axis=-1, keepdims=True)
    normed = (inputs32 * lax.rsqrt(mean_square + NORM_EPS) * input_gain.astype(F32)).astype(BF16)
    mine = lax.dynamic_slice_in_dim(normed, f * half, half, 1)
    theirs = swap(lax.dynamic_slice_in_dim(normed, (1 - f) * half, half, 1))

    message = jnp.concatenate([message[:-16], bound], axis=0)
    message, lower_near = lax.optimization_barrier((message, lower_near))
    upper_o = along_z(along_y(message))
    bound = jnp.max(upper_o[:, :, -16:]).astype(F32)

    weight_q, _ = lax.optimization_barrier((query_base_weight, lower_near))
    weight_q = fetch(weight_q, "fetch_query")
    half_done = query_project(0, t[None], lower_near, upper, weight_q, mine, theirs)
    query_effective, own, other = query_project(
        1, t[None], lower_far, upper, weight_q, mine, theirs, half_done
    )
    other = swap(other)

    inverse = ROPE_BASE ** (-(np.arange(head_dim // 2) * 2.0) / head_dim)
    inverse = jnp.asarray(inverse.astype(np.float32))
    positions = cache_lengths[:, None] - steps + jnp.arange(steps, dtype=jnp.int32)[None, :]
    angles = positions.astype(F32).reshape(tall, 1) * inverse
    cosine, sine = jnp.cos(angles), jnp.sin(angles)
    context = attend(
        cache_lengths,
        own,
        other,
        query_bias[None, :],
        jnp.concatenate([cosine, cosine], axis=1),
        jnp.concatenate([-sine, sine], axis=1),
        cache_keys[:, 0],
        cache_values[:, 0],
        steps,
        width ** (-0.5),
    )

    output_effective, own, other = output_project(
        t[None], lower_o, upper_o, output_base_weight, context, swap(context)
    )

    small = 2.0**-16
    unit = jnp.maximum(bound, 1e-30) * small
    shrink_by = 1.0 / unit

    def shrink(value):
        return (value * shrink_by) * (features ** (-0.5) * small)

    near, far = reduce_blocks(own, other, shrink)

    near = along_z(near)
    near = jnp.stack([near, hop(near, 1)], axis=1)
    far = along_z(far)
    near = near.reshape((2 * outer,) + near.shape[2:]).astype(F32)
    far = far.reshape((2 * outer,) + far.shape[2:]).astype(F32)

    residual, normed_out = finish(
        place, jnp.maximum(bound, 1e-30)[None], flat, post_gain[None, :], near, far
    )
    return (
        residual.reshape(hidden_in.shape),
        normed_out.reshape(hidden_in.shape),
        query_effective,
        output_effective,
    )


def solution(mesh):
    in_specs = (
        P(("groups", "fsdp"), None, None),
        P(),
        P(),
        P("fsdp", "tp"),
        P("tp"),
        P("tp", "fsdp"),
        P(("fsdp", "tp"), None),
        P("fsdp", "tp"),
        P("tp", "fsdp"),
        P(None, ("fsdp", "tp")),
        P(("groups", "fsdp"), "tp", None, None),
        P(("groups", "fsdp"), "tp", None, None),
        P(("groups", "fsdp")),
    )
    out_specs = (
        P(("groups", "fsdp"), None, None),
        P(("groups", "fsdp"), None, None),
        P(("groups", "fsdp"), "tp"),
        P(("groups", "tp"), "fsdp"),
    )
    return jax.shard_map(local, mesh=mesh, in_specs=in_specs, out_specs=out_specs, check_vma=False)
```

```python
import functools

import jax
import jax.numpy as jnp
import numpy as np
from jax import lax
from jax.experimental import pallas as pl
from jax.experimental.pallas import tpu as pltpu
from jax.sharding import PartitionSpec as P

NORM_EPS = 1e-06
ROPE_BASE = 1000000.0
ADAPTER_SCALE = 0.5
MIB = 1024 * 1024
BF16 = jnp.bfloat16
F16 = jnp.float16
F32 = jnp.float32
SWAP = [(0, 1), (1, 0)]


def params(room):
    return pltpu.CompilerParams(vmem_limit_bytes=room * MIB)


def cost(flops, read):
    return pl.CostEstimate(flops=flops, bytes_accessed=read, transcendentals=0)


def hop(value, distance):
    total = lax.axis_size("tp")
    return lax.ppermute(value, "tp", [(i, i ^ distance) for i in range(total)])


def swap(value):
    return lax.ppermute(value, "fsdp", SWAP)


def contract_first(left, right):
    return lax.dot_general(left, right, (((0,), (0,)), ((), ())), preferred_element_type=F32)


VMEM = pl.BlockSpec(memory_space=pltpu.VMEM)
SMEM = pl.BlockSpec(memory_space=pltpu.SMEM)
ANY = pl.BlockSpec(memory_space=pl.ANY)


def in_vmem(value):
    return pltpu.with_memory_space_constraint(value, pltpu.VMEM)


def in_hbm(value):
    return pltpu.with_memory_space_constraint(value, pltpu.HBM)


def fetch_kernel(source, target, arrived):
    copy = pltpu.make_async_copy(source, target, arrived)
    copy.start()
    copy.wait()


def fetch(value, name):
    return pl.pallas_call(
        fetch_kernel,
        in_specs=[ANY],
        out_specs=VMEM,
        out_shape=pltpu.VMEM(value.shape, value.dtype),
        scratch_shapes=[pltpu.SemaphoreType.DMA],
        compiler_params=params(2),
        cost_estimate=cost(0, 2 * value.size),
        name=name,
    )(in_hbm(value))


def reach_kernel(lengths, values, upper, message, held, arrived, factor, factor_arrived):
    rows, slots, head_dim = values.shape
    rank, width = upper.shape
    copies = [
        pltpu.make_async_copy(values.at[row], held.at[row], arrived.at[row]) for row in range(rows)
    ]
    columns = pltpu.make_async_copy(upper, factor, factor_arrived)
    columns.start()
    for copy in copies:
        copy.start()
    part = 256
    slot = lax.broadcasted_iota(jnp.int32, (part, head_dim), 0)
    top = jnp.zeros((16, head_dim), BF16)
    edge = jnp.zeros((8, head_dim), F32)
    for row in range(rows):
        copies[row].wait()
        whole = lengths[row] // part

        def full(n, top, row=row):
            size = jnp.abs(held[row, pl.ds(pl.multiple_of(n * part, part), part)])
            return jnp.maximum(top, jnp.max(size.reshape(-1, 16, head_dim), axis=0))

        top = lax.fori_loop(0, whole, full, top)
        last = pl.multiple_of(jnp.minimum(whole, slots // part - 1) * part, part)
        size = jnp.abs(held[row, pl.ds(last, part)].astype(F32))
        size = jnp.where(slot < lengths[row] - last, size, 0.0)
        edge = jnp.maximum(edge, jnp.max(size.reshape(-1, 8, head_dim), axis=0))
    most = jnp.maximum(jnp.max(top.astype(F32)), jnp.max(edge))
    columns.wait()
    for first in range(0, width, 128):
        message[first // 128 * rank : (first // 128 + 1) * rank] = factor[:, first : first + 128]
    message[width // 128 * rank :] = jnp.broadcast_to(most, (16, 128)).astype(BF16)


def with_largest_in_reach(lengths, values, upper):
    rank, width = upper.shape
    return pl.pallas_call(
        reach_kernel,
        in_specs=[SMEM, ANY, ANY],
        out_specs=VMEM,
        out_shape=jax.ShapeDtypeStruct((width // 128 * rank + 16, 128), BF16),
        scratch_shapes=[
            pltpu.VMEM(values.shape, BF16),
            pltpu.SemaphoreType.DMA((values.shape[0],)),
            pltpu.VMEM(upper.shape, BF16),
            pltpu.SemaphoreType.DMA,
        ],
        compiler_params=params(8),
        cost_estimate=cost(4 * values.size, 2 * values.size),
        name="with_largest_in_reach",
    )(lengths, in_hbm(values), in_hbm(upper))


def query_kernel(y, place, lower, upper, base, mine, theirs, *refs):
    before, (effective, own, other, fresh, total, left) = refs[: 3 * y], refs[3 * y :]
    outer, _, depth = lower.shape
    rows = mine.shape[0]
    if y:
        total[:rows] = before[1][...]
        total[rows:] = before[2][...]
    else:
        total[...] = jnp.zeros_like(total)

    def pair(half, _):
        for slot in range(2):
            z = 2 * half + slot
            start = pl.multiple_of(((2 * z + y) ^ place[0]) * depth, depth)
            block = pl.ds(start, depth)
            out = pltpu.make_async_copy(fresh.at[slot], effective.at[block], left.at[slot])

            @pl.when(half > 0)
            def _():
                out.wait()

            update = contract_first(lower[z], upper[...])
            fresh[slot] = (base[block, :].astype(F32) + update).astype(BF16)
            out.start()
            both = jnp.concatenate([mine[:, block], theirs[:, block]], axis=0)
            total[...] += jnp.dot(both, fresh[slot], preferred_element_type=F32)
        return 0

    lax.fori_loop(0, outer // 2, pair, 0)
    own[...] = total[:rows]
    other[...] = total[rows:]
    for slot in range(2):
        pltpu.make_async_copy(
            fresh.at[slot], effective.at[pl.ds(0, depth)], left.at[slot]
        ).wait()


def query_project(y, place, lower, upper, base, mine, theirs, before=()):
    depth = lower.shape[2]
    width = base.shape[1]
    rows = mine.shape[0]
    return pl.pallas_call(
        functools.partial(query_kernel, y),
        in_specs=[SMEM] + [VMEM] * 5 + [ANY, VMEM, VMEM][: len(before)],
        out_specs=[ANY, VMEM, VMEM],
        out_shape=[
            jax.ShapeDtypeStruct(base.shape, BF16),
            jax.ShapeDtypeStruct((rows, width), F32),
            jax.ShapeDtypeStruct((rows, width), F32),
        ],
        scratch_shapes=[
            pltpu.VMEM((2, depth, width), BF16),
            pltpu.VMEM((2 * rows, width), F32),
            pltpu.SemaphoreType.DMA((2,)),
        ],
        input_output_aliases={6: 0} if before else {},
        compiler_params=params(14),
        cost_estimate=cost(base.size * (lower.shape[1] + 2 * rows), base.size),
        name="query_project",
    )(place, lower, upper, in_vmem(base), mine, theirs, *before)


def attend_kernel(
    steps, scale, lengths, own, other, bias, cosine, sine, keys, values, context,
    keys_held, values_held, arrived
):
    rows, slots, head_dim = keys.shape
    heads = own.shape[1] // head_dim
    copies = []
    for row in range(rows):
        copies.append(
            [
                pltpu.make_async_copy(keys.at[row], keys_held.at[row], arrived.at[0, row]),
                pltpu.make_async_copy(values.at[row], values_held.at[row], arrived.at[1, row]),
            ]
        )
        for copy in copies[row]:
            copy.start()
    slot = lax.broadcasted_iota(jnp.int32, (heads * steps, slots), 1)
    step = lax.broadcasted_iota(jnp.int32, (heads * steps, slots), 0) % steps
    behind = slot - step
    many = heads * steps
    nothing = jnp.zeros((many, head_dim), F32)
    for first in range(0, rows, 2):
        pair = (first, first + 1)
        span = slice(first * steps, (first + 2) * steps)
        query = (own[span] + other[span]) * scale + bias[...].astype(F32)
        turned = []
        for head in range(heads):
            part = query[:, head * head_dim : (head + 1) * head_dim]
            part = part * cosine[span] + pltpu.roll(part, head_dim // 2, 1) * sine[span]
            turned.append(part * head_dim ** (-0.5))
        upper, lower = [
            jnp.concatenate([q[i * steps : (i + 1) * steps] for q in turned], axis=0) for i in (0, 1)
        ]
        queries = jnp.concatenate(
            [
                jnp.concatenate([upper, nothing], axis=1),
                jnp.concatenate([nothing, lower], axis=1),
            ],
            axis=0,
        ).astype(BF16)
        for row in pair:
            copies[row][0].wait()
        both = jnp.concatenate([keys_held[row] for row in pair], axis=1)
        scores = lax.dot_general(
            queries, both, (((1,), (1,)), ((), ())), preferred_element_type=F32
        )
        scores = jnp.concatenate(
            [
                jnp.where(
                    behind <= lengths[first + i] - steps,
                    scores[i * many : (i + 1) * many],
                    F32(-1e30),
                )
                for i in (0, 1)
            ],
            axis=0,
        )
        top = jnp.max(scores, axis=-1, keepdims=True)
        weights = jnp.exp(scores - top)
        probs = (weights / jnp.sum(weights, axis=-1, keepdims=True)).astype(BF16)
        for row in pair:
            copies[row][1].wait()
        both = jnp.concatenate([values_held[row] for row in pair], axis=1)
        mixed = jnp.dot(probs, both, preferred_element_type=F32)
        gathered = (mixed[:many, :head_dim], mixed[many:, head_dim:])
        for head in range(heads):
            context[span, head * head_dim : (head + 1) * head_dim] = jnp.concatenate(
                [g[head * steps : (head + 1) * steps] for g in gathered], axis=0
            ).astype(BF16)


def attend(lengths, own, other, bias, cosine, sine, keys, values, steps, scale):
    rows = keys.shape[0]
    width = own.shape[1]
    return pl.pallas_call(
        functools.partial(attend_kernel, steps, scale),
        in_specs=[SMEM] + [VMEM] * 5 + [ANY] * 2,
        out_specs=VMEM,
        out_shape=jax.ShapeDtypeStruct((rows * steps, width), BF16),
        scratch_shapes=[
            pltpu.VMEM(keys.shape, BF16),
            pltpu.VMEM(values.shape, BF16),
            pltpu.SemaphoreType.DMA((2, rows)),
        ],
        compiler_params=params(18),
        cost_estimate=cost(4 * keys.size * width // keys.shape[2] * steps, 4 * keys.size),
        name="attend",
    )(lengths, own, other, bias, cosine, sine, in_hbm(keys), in_hbm(values))


def output_kernel(
    place, lower, upper, base, mine, theirs, effective, own, other, held, fresh, arrived, left
):
    outer = upper.shape[0]
    rank = lower.shape[0]
    width = fresh.shape[2]
    rows = mine.shape[0]

    def columns(k):
        return pl.ds(pl.multiple_of((k ^ place[0]) * width, width), width)

    def fetch(k):
        return pltpu.make_async_copy(base.at[:, columns(k)], held.at[k], arrived.at[k])

    def ask(k, _):
        fetch(k).start()
        return 0

    lax.fori_loop(0, 2 * outer, ask, 0)
    both = jnp.concatenate([mine[...], theirs[...]], axis=0)

    def pair(z, _):
        for y in range(2):
            k = 2 * z + y
            out = pltpu.make_async_copy(fresh.at[y], effective.at[:, columns(k)], left.at[y])

            @pl.when(z > 0)
            def _():
                out.wait()

            factor = [upper[lax.rem(outer - z, outer), y, n * rank : (n + 1) * rank] for n in range(width // 128)]
            update = contract_first(lower[...], jnp.concatenate(factor, axis=1))
            fetch(k).wait()
            fresh[y] = (held[k].astype(F32) + update).astype(BF16)
            out.start()
            product = jnp.dot(both, fresh[y], preferred_element_type=F32)
            own[y, z] = product[:rows]
            other[z, y] = product[rows:]
        return 0

    lax.fori_loop(0, outer, pair, 0)
    for y in range(2):
        pltpu.make_async_copy(fresh.at[y], effective.at[:, pl.ds(0, width)], left.at[y]).wait()


def output_project(place, lower, upper, base, mine, theirs):
    outer = upper.shape[0]
    width = base.shape[1] // (2 * outer)
    depth = base.shape[0]
    rows = mine.shape[0]
    return pl.pallas_call(
        output_kernel,
        in_specs=[SMEM, VMEM, VMEM, ANY, VMEM, VMEM],
        out_specs=[ANY, VMEM, VMEM],
        out_shape=[
            jax.ShapeDtypeStruct(base.shape, BF16),
            jax.ShapeDtypeStruct((2, outer, rows, width), F32),
            jax.ShapeDtypeStruct((outer, 2, rows, width), F32),
        ],
        scratch_shapes=[
            pltpu.VMEM((2 * outer, depth, width), BF16),
            pltpu.VMEM((2, depth, width), BF16),
            pltpu.SemaphoreType.DMA((2 * outer,)),
            pltpu.SemaphoreType.DMA((2,)),
        ],
        compiler_params=params(24),
        cost_estimate=cost(2 * base.size * (lower.shape[0] + 2 * rows), 4 * base.size),
        name="output_project",
    )(place, lower, upper, in_hbm(base), mine, theirs)


def finish_kernel(place, bound, hidden, gain, near, far, residual, normed, combined, held, left):
    blocks, rows, width = near.shape
    half = blocks * width
    tall = combined.shape[0]

    def put(which, out, first):
        slot = first // tall % 2
        return pltpu.make_async_copy(
            held.at[which, slot], out.at[pl.ds(first, tall)], left.at[which, slot]
        )

    for first in range(0, rows, tall):
        slot = first // tall % 2
        if first >= 2 * tall:
            put(0, residual, first - 2 * tall).wait()
            put(1, normed, first - 2 * tall).wait()
        squares = jnp.zeros((tall, 128), F32)
        for pieces, which in ((near, place[1]), (far, 1 - place[1])):
            for k in range(blocks):
                start = pl.multiple_of(which * half + (place[0] ^ k) * width, width)
                total = hidden[first : first + tall, pl.ds(start, width)].astype(F32)
                total += pieces[k, first : first + tall] * bound[0]
                combined[:, pl.ds(start, width)] = total
                held[0, slot, :, pl.ds(start, width)] = total.astype(BF16)
                for lane in range(0, width, 128):
                    squares += total[:, lane : lane + 128] * total[:, lane : lane + 128]
        put(0, residual, first).start()
        mean = jnp.sum(squares, axis=-1, keepdims=True) / (2 * half)
        inverse = lax.rsqrt(mean + NORM_EPS)
        held[1, slot] = (combined[...] * inverse * gain[...].astype(F32)).astype(BF16)
        put(1, normed, first).start()
    for first in range(max(rows - 2 * tall, 0), rows, tall):
        put(0, residual, first).wait()
        put(1, normed, first).wait()


def finish(place, bound, hidden, gain, near, far):
    rows, whole = hidden.shape
    tall = 16
    return pl.pallas_call(
        finish_kernel,
        in_specs=[SMEM, SMEM] + [VMEM] * 4,
        out_specs=[ANY, ANY],
        out_shape=[jax.ShapeDtypeStruct((rows, whole), BF16)] * 2,
        scratch_shapes=[
            pltpu.VMEM((tall, whole), F32),
            pltpu.VMEM((2, 2, tall, whole), BF16),
            pltpu.SemaphoreType.DMA((2, 2)),
        ],
        compiler_params=params(14),
        cost_estimate=cost(8 * hidden.size, 14 * hidden.size),
        name="finish",
    )(place, bound, hidden, gain, near, far)


def cross(value):
    total = lax.axis_size("tp")
    pairs = [(f * total + i, (1 - f) * total + (i ^ 1)) for f in range(2) for i in range(total)]
    return lax.ppermute(value, ("fsdp", "tp"), pairs)


def along_z(value):
    outer = lax.axis_size("tp") // 2
    return jnp.stack([value] + [hop(value, 2 * k) for k in range(1, outer)])


def along_z_far_first(value):
    outer = lax.axis_size("tp") // 2
    return jnp.stack([value] + [hop(value, 2 * k) for k in range(outer - 1, 0, -1)])


def along_y(value):
    return jnp.stack([value, hop(value, 1)])


def reduce_blocks(own, other, shrink):
    outer = other.shape[0]

    def narrow(value):
        return value.astype(F16)

    across = hop(narrow(shrink(own[1])), 1)
    arrived = [hop(narrow(shrink(other[k])), 2 * k) for k in range(outer - 1, 0, -1)]
    summed = shrink(own[0]) + across.astype(F32)
    ended = [hop(narrow(summed[k]), 2 * k) for k in range(1, outer)]
    arrived, ended[:1] = lax.optimization_barrier((arrived, ended[:1]))
    total = summed[0] + sum(e.astype(F32) for e in ended)
    pair = narrow(shrink(other[0]) + sum(a.astype(F32) for a in arrived))
    far = swap(pair).astype(F32) + cross(pair)[::-1].astype(F32)
    return narrow(total), narrow(far)


def local(
    hidden_in,
    input_gain,
    post_gain,
    query_base_weight,
    query_bias,
    output_base_weight,
    query_lower_factor,
    query_upper_factor,
    output_lower_factor,
    output_upper_factor,
    cache_keys,
    cache_values,
    cache_lengths,
):
    rows, steps, width = hidden_in.shape
    tall = rows * steps
    half = width // 2
    slots, head_dim = cache_keys.shape[2:]
    features = query_base_weight.shape[1] * lax.axis_size("tp")
    t = lax.axis_index("tp").astype(jnp.int32)
    f = lax.axis_index("fsdp").astype(jnp.int32)
    place = jnp.stack([t, f])
    outer = lax.axis_size("tp") // 2

    lower_near = along_z(query_lower_factor.T)
    lower_far = hop(lower_near, 1)

    rank_part = query_upper_factor.shape[0]
    sent = jnp.concatenate([query_upper_factor, output_lower_factor.T], axis=0)
    came = swap(sent)

    def in_order(a, b):
        return jnp.where(f == 0, jnp.concatenate([a, b]), jnp.concatenate([b, a]))

    upper = in_order(sent[:rank_part], came[:rank_part]) * BF16(ADAPTER_SCALE)
    lower_o = in_order(sent[rank_part:], came[rank_part:]) * BF16(ADAPTER_SCALE)

    message = with_largest_in_reach(cache_lengths, cache_values[:, 0], output_upper_factor)
    bound = jnp.maximum(message[-16:], swap(message[-16:]))

    hidden, message = lax.optimization_barrier((hidden_in, message))
    flat = hidden.reshape(tall, width)
    inputs32 = flat.astype(F32)
    mean_square = jnp.mean(inputs32 * inputs32, axis=-1, keepdims=True)
    normed = (inputs32 * lax.rsqrt(mean_square + NORM_EPS) * input_gain.astype(F32)).astype(BF16)
    mine = lax.dynamic_slice_in_dim(normed, f * half, half, 1)
    theirs = swap(lax.dynamic_slice_in_dim(normed, (1 - f) * half, half, 1))

    message = jnp.concatenate([message[:-16], bound], axis=0)
    message, lower_near = lax.optimization_barrier((message, lower_near))
    upper_o = along_z_far_first(along_y(message))
    bound = jnp.max(upper_o[:, :, -16:]).astype(F32)

    weight_q, _ = lax.optimization_barrier((query_base_weight, lower_near))
    weight_q = fetch(weight_q, "fetch_query")
    half_done = query_project(0, t[None], lower_near, upper, weight_q, mine, theirs)
    query_effective, own, other = query_project(
        1, t[None], lower_far, upper, weight_q, mine, theirs, half_done
    )
    other = swap(other)

    inverse = ROPE_BASE ** (-(np.arange(head_dim // 2) * 2.0) / head_dim)
    inverse = jnp.asarray(inverse.astype(np.float32))
    positions = cache_lengths[:, None] - steps + jnp.arange(steps, dtype=jnp.int32)[None, :]
    angles = positions.astype(F32).reshape(tall, 1) * inverse
    cosine, sine = jnp.cos(angles), jnp.sin(angles)
    context = attend(
        cache_lengths,
        own,
        other,
        query_bias[None, :],
        jnp.concatenate([cosine, cosine], axis=1),
        jnp.concatenate([-sine, sine], axis=1),
        cache_keys[:, 0],
        cache_values[:, 0],
        steps,
        width ** (-0.5),
    )

    output_effective, own, other = output_project(
        t[None], lower_o, upper_o, output_base_weight, context, swap(context)
    )

    small = 2.0**-16
    unit = jnp.maximum(bound, 1e-30) * small
    shrink_by = 1.0 / unit

    def shrink(value):
        return (value * shrink_by) * (features ** (-0.5) * small)

    near, far = reduce_blocks(own, other, shrink)

    near = along_z(near)
    near = jnp.stack([near, hop(near, 1)], axis=1)
    far = along_z(far)
    near = near.reshape((2 * outer,) + near.shape[2:]).astype(F32)
    far = far.reshape((2 * outer,) + far.shape[2:]).astype(F32)

    residual, normed_out = finish(
        place, jnp.maximum(bound, 1e-30)[None], flat, post_gain[None, :], near, far
    )
    return (
        residual.reshape(hidden_in.shape),
        normed_out.reshape(hidden_in.shape),
        query_effective,
        output_effective,
    )


def solution(mesh):
    in_specs = (
        P(("groups", "fsdp"), None, None),
        P(),
        P(),
        P("fsdp", "tp"),
        P("tp"),
        P("tp", "fsdp"),
        P(("fsdp", "tp"), None),
        P("fsdp", "tp"),
        P("tp", "fsdp"),
        P(None, ("fsdp", "tp")),
        P(("groups", "fsdp"), "tp", None, None),
        P(("groups", "fsdp"), "tp", None, None),
        P(("groups", "fsdp")),
    )
    out_specs = (
        P(("groups", "fsdp"), None, None),
        P(("groups", "fsdp"), None, None),
        P(("groups", "fsdp"), "tp"),
        P(("groups", "tp"), "fsdp"),
    )
    return jax.shard_map(local, mesh=mesh, in_specs=in_specs, out_specs=out_specs, check_vma=False)
```

```python
import functools

import jax
import jax.numpy as jnp
import numpy as np
from jax import lax
from jax.experimental import pallas as pl
from jax.experimental.pallas import tpu as pltpu
from jax.sharding import PartitionSpec as P

NORM_EPS = 1e-06
ROPE_BASE = 1000000.0
ADAPTER_SCALE = 0.5
MIB = 1024 * 1024
BF16 = jnp.bfloat16
F16 = jnp.float16
F32 = jnp.float32
SWAP = [(0, 1), (1, 0)]


def params(room):
    return pltpu.CompilerParams(vmem_limit_bytes=room * MIB)


def cost(flops, read):
    return pl.CostEstimate(flops=flops, bytes_accessed=read, transcendentals=0)


def hop(value, distance):
    total = lax.axis_size("tp")
    return lax.ppermute(value, "tp", [(i, i ^ distance) for i in range(total)])


def swap(value):
    return lax.ppermute(value, "fsdp", SWAP)


def contract_first(left, right):
    return lax.dot_general(left, right, (((0,), (0,)), ((), ())), preferred_element_type=F32)


VMEM = pl.BlockSpec(memory_space=pltpu.VMEM)
SMEM = pl.BlockSpec(memory_space=pltpu.SMEM)
ANY = pl.BlockSpec(memory_space=pl.ANY)


def in_vmem(value):
    return pltpu.with_memory_space_constraint(value, pltpu.VMEM)


def in_hbm(value):
    return pltpu.with_memory_space_constraint(value, pltpu.HBM)


def fetch_kernel(source, target, arrived):
    copy = pltpu.make_async_copy(source, target, arrived)
    copy.start()
    copy.wait()


def fetch(value, name):
    return pl.pallas_call(
        fetch_kernel,
        in_specs=[ANY],
        out_specs=VMEM,
        out_shape=pltpu.VMEM(value.shape, value.dtype),
        scratch_shapes=[pltpu.SemaphoreType.DMA],
        compiler_params=params(2),
        cost_estimate=cost(0, 2 * value.size),
        name=name,
    )(in_hbm(value))


def reach_kernel(lengths, values, upper, message, held, arrived, factor, factor_arrived):
    rows, slots, head_dim = values.shape
    rank, width = upper.shape
    copies = [
        pltpu.make_async_copy(values.at[row], held.at[row], arrived.at[row]) for row in range(rows)
    ]
    columns = pltpu.make_async_copy(upper, factor, factor_arrived)
    columns.start()
    for copy in copies:
        copy.start()
    part = 256
    slot = lax.broadcasted_iota(jnp.int32, (part, head_dim), 0)
    top = jnp.zeros((16, head_dim), BF16)
    edge = jnp.zeros((8, head_dim), F32)
    for row in range(rows):
        copies[row].wait()
        whole = lengths[row] // part

        def full(n, top, row=row):
            size = jnp.abs(held[row, pl.ds(pl.multiple_of(n * part, part), part)])
            return jnp.maximum(top, jnp.max(size.reshape(-1, 16, head_dim), axis=0))

        top = lax.fori_loop(0, whole, full, top)
        last = pl.multiple_of(jnp.minimum(whole, slots // part - 1) * part, part)
        size = jnp.abs(held[row, pl.ds(last, part)].astype(F32))
        size = jnp.where(slot < lengths[row] - last, size, 0.0)
        edge = jnp.maximum(edge, jnp.max(size.reshape(-1, 8, head_dim), axis=0))
    most = jnp.maximum(jnp.max(top.astype(F32)), jnp.max(edge))
    columns.wait()
    for first in range(0, width, 128):
        message[first // 128 * rank : (first // 128 + 1) * rank] = factor[:, first : first + 128]
    message[width // 128 * rank :] = jnp.broadcast_to(most, (16, 128)).astype(BF16)


def with_largest_in_reach(lengths, values, upper):
    rank, width = upper.shape
    return pl.pallas_call(
        reach_kernel,
        in_specs=[SMEM, ANY, ANY],
        out_specs=VMEM,
        out_shape=jax.ShapeDtypeStruct((width // 128 * rank + 16, 128), BF16),
        scratch_shapes=[
            pltpu.VMEM(values.shape, BF16),
            pltpu.SemaphoreType.DMA((values.shape[0],)),
            pltpu.VMEM(upper.shape, BF16),
            pltpu.SemaphoreType.DMA,
        ],
        compiler_params=params(8),
        cost_estimate=cost(4 * values.size, 2 * values.size),
        name="with_largest_in_reach",
    )(lengths, in_hbm(values), in_hbm(upper))


def query_kernel(y, place, lower, upper, base, mine, theirs, *refs):
    before, (effective, own, other, fresh, total, left) = refs[: 3 * y], refs[3 * y :]
    outer, _, depth = lower.shape
    rows = mine.shape[0]
    if y:
        total[:rows] = before[1][...]
        total[rows:] = before[2][...]
    else:
        total[...] = jnp.zeros_like(total)

    def pair(half, _):
        for slot in range(2):
            z = 2 * half + slot
            start = pl.multiple_of(((2 * z + y) ^ place[0]) * depth, depth)
            block = pl.ds(start, depth)
            out = pltpu.make_async_copy(fresh.at[slot], effective.at[block], left.at[slot])

            @pl.when(half > 0)
            def _():
                out.wait()

            update = contract_first(lower[z], upper[...])
            fresh[slot] = (base[block, :].astype(F32) + update).astype(BF16)
            out.start()
            both = jnp.concatenate([mine[:, block], theirs[:, block]], axis=0)
            total[...] += jnp.dot(both, fresh[slot], preferred_element_type=F32)
        return 0

    lax.fori_loop(0, outer // 2, pair, 0)
    own[...] = total[:rows]
    other[...] = total[rows:]
    for slot in range(2):
        pltpu.make_async_copy(
            fresh.at[slot], effective.at[pl.ds(0, depth)], left.at[slot]
        ).wait()


def query_project(y, place, lower, upper, base, mine, theirs, before=()):
    depth = lower.shape[2]
    width = base.shape[1]
    rows = mine.shape[0]
    return pl.pallas_call(
        functools.partial(query_kernel, y),
        in_specs=[SMEM] + [VMEM] * 5 + [ANY, VMEM, VMEM][: len(before)],
        out_specs=[ANY, VMEM, VMEM],
        out_shape=[
            jax.ShapeDtypeStruct(base.shape, BF16),
            jax.ShapeDtypeStruct((rows, width), F32),
            jax.ShapeDtypeStruct((rows, width), F32),
        ],
        scratch_shapes=[
            pltpu.VMEM((2, depth, width), BF16),
            pltpu.VMEM((2 * rows, width), F32),
            pltpu.SemaphoreType.DMA((2,)),
        ],
        input_output_aliases={6: 0} if before else {},
        compiler_params=params(14),
        cost_estimate=cost(base.size * (lower.shape[1] + 2 * rows), base.size),
        name="query_project",
    )(place, lower, upper, in_vmem(base), mine, theirs, *before)


def attend_kernel(
    steps, scale, lengths, own, other, bias, cosine, sine, keys, values, context,
    keys_held, values_held, arrived
):
    rows, slots, head_dim = keys.shape
    heads = own.shape[1] // head_dim
    copies = []
    for row in range(rows):
        copies.append(
            [
                pltpu.make_async_copy(keys.at[row], keys_held.at[row], arrived.at[0, row]),
                pltpu.make_async_copy(values.at[row], values_held.at[row], arrived.at[1, row]),
            ]
        )
        for copy in copies[row]:
            copy.start()
    slot = lax.broadcasted_iota(jnp.int32, (heads * steps, slots), 1)
    step = lax.broadcasted_iota(jnp.int32, (heads * steps, slots), 0) % steps
    behind = slot - step
    many = heads * steps
    nothing = jnp.zeros((many, head_dim), F32)
    for first in range(0, rows, 2):
        pair = (first, first + 1)
        span = slice(first * steps, (first + 2) * steps)
        query = (own[span] + other[span]) * scale + bias[...].astype(F32)
        turned = []
        for head in range(heads):
            part = query[:, head * head_dim : (head + 1) * head_dim]
            part = part * cosine[span] + pltpu.roll(part, head_dim // 2, 1) * sine[span]
            turned.append(part * head_dim ** (-0.5))
        upper, lower = [
            jnp.concatenate([q[i * steps : (i + 1) * steps] for q in turned], axis=0) for i in (0, 1)
        ]
        queries = jnp.concatenate(
            [
                jnp.concatenate([upper, nothing], axis=1),
                jnp.concatenate([nothing, lower], axis=1),
            ],
            axis=0,
        ).astype(BF16)
        for row in pair:
            copies[row][0].wait()
        both = jnp.concatenate([keys_held[row] for row in pair], axis=1)
        scores = lax.dot_general(
            queries, both, (((1,), (1,)), ((), ())), preferred_element_type=F32
        )
        scores = jnp.concatenate(
            [
                jnp.where(
                    behind <= lengths[first + i] - steps,
                    scores[i * many : (i + 1) * many],
                    F32(-1e30),
                )
                for i in (0, 1)
            ],
            axis=0,
        )
        top = jnp.max(scores, axis=-1, keepdims=True)
        weights = jnp.exp(scores - top)
        probs = (weights / jnp.sum(weights, axis=-1, keepdims=True)).astype(BF16)
        for row in pair:
            copies[row][1].wait()
        both = jnp.concatenate([values_held[row] for row in pair], axis=1)
        mixed = jnp.dot(probs, both, preferred_element_type=F32)
        gathered = (mixed[:many, :head_dim], mixed[many:, head_dim:])
        for head in range(heads):
            context[span, head * head_dim : (head + 1) * head_dim] = jnp.concatenate(
                [g[head * steps : (head + 1) * steps] for g in gathered], axis=0
            ).astype(BF16)


def attend(lengths, own, other, bias, cosine, sine, keys, values, steps, scale):
    rows = keys.shape[0]
    width = own.shape[1]
    return pl.pallas_call(
        functools.partial(attend_kernel, steps, scale),
        in_specs=[SMEM] + [VMEM] * 5 + [ANY] * 2,
        out_specs=VMEM,
        out_shape=jax.ShapeDtypeStruct((rows * steps, width), BF16),
        scratch_shapes=[
            pltpu.VMEM(keys.shape, BF16),
            pltpu.VMEM(values.shape, BF16),
            pltpu.SemaphoreType.DMA((2, rows)),
        ],
        compiler_params=params(18),
        cost_estimate=cost(4 * keys.size * width // keys.shape[2] * steps, 4 * keys.size),
        name="attend",
    )(lengths, own, other, bias, cosine, sine, in_hbm(keys), in_hbm(values))


def output_kernel(
    place, lower, upper, base, mine, theirs, effective, own, other, held, fresh, arrived, left
):
    outer = upper.shape[0]
    rank = lower.shape[0]
    width = fresh.shape[2]
    rows = mine.shape[0]

    def columns(k):
        return pl.ds(pl.multiple_of((k ^ place[0]) * width, width), width)

    def fetch(k):
        return pltpu.make_async_copy(base.at[:, columns(k)], held.at[k], arrived.at[k])

    def ask(k, _):
        fetch(k).start()
        return 0

    lax.fori_loop(0, 2 * outer, ask, 0)
    both = jnp.concatenate([mine[...], theirs[...]], axis=0)

    def pair(z, _):
        for y in range(2):
            k = 2 * z + y
            out = pltpu.make_async_copy(fresh.at[y], effective.at[:, columns(k)], left.at[y])

            @pl.when(z > 0)
            def _():
                out.wait()

            factor = [upper[lax.rem(outer - z, outer), y, n * rank : (n + 1) * rank] for n in range(width // 128)]
            update = contract_first(lower[...], jnp.concatenate(factor, axis=1))
            fetch(k).wait()
            fresh[y] = (held[k].astype(F32) + update).astype(BF16)
            out.start()
            product = jnp.dot(both, fresh[y], preferred_element_type=F32)
            own[y, z] = product[:rows]
            other[z, y] = product[rows:]
        return 0

    lax.fori_loop(0, outer, pair, 0)
    for y in range(2):
        pltpu.make_async_copy(fresh.at[y], effective.at[:, pl.ds(0, width)], left.at[y]).wait()


def output_project(place, lower, upper, base, mine, theirs):
    outer = upper.shape[0]
    width = base.shape[1] // (2 * outer)
    depth = base.shape[0]
    rows = mine.shape[0]
    return pl.pallas_call(
        output_kernel,
        in_specs=[SMEM, VMEM, VMEM, ANY, VMEM, VMEM],
        out_specs=[ANY, VMEM, VMEM],
        out_shape=[
            jax.ShapeDtypeStruct(base.shape, BF16),
            jax.ShapeDtypeStruct((2, outer, rows, width), F32),
            jax.ShapeDtypeStruct((outer, 2, rows, width), F32),
        ],
        scratch_shapes=[
            pltpu.VMEM((2 * outer, depth, width), BF16),
            pltpu.VMEM((2, depth, width), BF16),
            pltpu.SemaphoreType.DMA((2 * outer,)),
            pltpu.SemaphoreType.DMA((2,)),
        ],
        compiler_params=params(24),
        cost_estimate=cost(2 * base.size * (lower.shape[0] + 2 * rows), 4 * base.size),
        name="output_project",
    )(place, lower, upper, in_hbm(base), mine, theirs)


def finish_kernel(place, bound, hidden, gain, near, far, residual, normed, combined, held, left):
    blocks, rows, width = near.shape
    half = blocks * width
    tall = combined.shape[0]

    def put(which, out, first):
        slot = first // tall % 2
        return pltpu.make_async_copy(
            held.at[which, slot], out.at[pl.ds(first, tall)], left.at[which, slot]
        )

    for first in range(0, rows, tall):
        slot = first // tall % 2
        if first >= 2 * tall:
            put(0, residual, first - 2 * tall).wait()
            put(1, normed, first - 2 * tall).wait()
        squares = jnp.zeros((tall, 128), F32)
        for pieces, which in ((near, place[1]), (far, 1 - place[1])):
            for k in range(blocks):
                at = (blocks - k // 2 * 2) % blocks + k % 2 if pieces is near else k
                start = pl.multiple_of(which * half + (place[0] ^ at) * width, width)
                total = hidden[first : first + tall, pl.ds(start, width)].astype(F32)
                total += pieces[k, first : first + tall] * bound[0]
                combined[:, pl.ds(start, width)] = total
                held[0, slot, :, pl.ds(start, width)] = total.astype(BF16)
                for lane in range(0, width, 128):
                    squares += total[:, lane : lane + 128] * total[:, lane : lane + 128]
        put(0, residual, first).start()
        mean = jnp.sum(squares, axis=-1, keepdims=True) / (2 * half)
        inverse = lax.rsqrt(mean + NORM_EPS)
        held[1, slot] = (combined[...] * inverse * gain[...].astype(F32)).astype(BF16)
        put(1, normed, first).start()
    for first in range(max(rows - 2 * tall, 0), rows, tall):
        put(0, residual, first).wait()
        put(1, normed, first).wait()


def finish(place, bound, hidden, gain, near, far):
    rows, whole = hidden.shape
    tall = 16
    return pl.pallas_call(
        finish_kernel,
        in_specs=[SMEM, SMEM] + [VMEM] * 4,
        out_specs=[ANY, ANY],
        out_shape=[jax.ShapeDtypeStruct((rows, whole), BF16)] * 2,
        scratch_shapes=[
            pltpu.VMEM((tall, whole), F32),
            pltpu.VMEM((2, 2, tall, whole), BF16),
            pltpu.SemaphoreType.DMA((2, 2)),
        ],
        compiler_params=params(14),
        cost_estimate=cost(8 * hidden.size, 14 * hidden.size),
        name="finish",
    )(place, bound, hidden, gain, near, far)


def cross(value):
    total = lax.axis_size("tp")
    pairs = [(f * total + i, (1 - f) * total + (i ^ 1)) for f in range(2) for i in range(total)]
    return lax.ppermute(value, ("fsdp", "tp"), pairs)


def along_z(value):
    outer = lax.axis_size("tp") // 2
    return jnp.stack([value] + [hop(value, 2 * k) for k in range(1, outer)])


def along_z_far_first(value):
    outer = lax.axis_size("tp") // 2
    return jnp.stack([value] + [hop(value, 2 * k) for k in range(outer - 1, 0, -1)])


def along_y(value):
    return jnp.stack([value, hop(value, 1)])


def reduce_blocks(own, other, shrink):
    outer = other.shape[0]

    def narrow(value):
        return value.astype(F16)

    across = hop(narrow(shrink(own[1])), 1)
    arrived = [hop(narrow(shrink(other[k])), 2 * k) for k in range(outer - 1, 0, -1)]
    summed = shrink(own[0]) + across.astype(F32)
    ended = [hop(narrow(summed[k]), 2 * k) for k in range(1, outer)]
    arrived, ended[:1] = lax.optimization_barrier((arrived, ended[:1]))
    total = summed[0] + sum(e.astype(F32) for e in ended)
    pair = narrow(shrink(other[0]) + sum(a.astype(F32) for a in arrived))
    far = swap(pair).astype(F32) + cross(pair)[::-1].astype(F32)
    return narrow(total), narrow(far)


def local(
    hidden_in,
    input_gain,
    post_gain,
    query_base_weight,
    query_bias,
    output_base_weight,
    query_lower_factor,
    query_upper_factor,
    output_lower_factor,
    output_upper_factor,
    cache_keys,
    cache_values,
    cache_lengths,
):
    rows, steps, width = hidden_in.shape
    tall = rows * steps
    half = width // 2
    slots, head_dim = cache_keys.shape[2:]
    features = query_base_weight.shape[1] * lax.axis_size("tp")
    t = lax.axis_index("tp").astype(jnp.int32)
    f = lax.axis_index("fsdp").astype(jnp.int32)
    place = jnp.stack([t, f])
    outer = lax.axis_size("tp") // 2

    lower_near = along_z(query_lower_factor.T)
    lower_far = hop(lower_near, 1)

    rank_part = query_upper_factor.shape[0]
    sent = jnp.concatenate([query_upper_factor, output_lower_factor.T], axis=0)
    came = swap(sent)

    def in_order(a, b):
        return jnp.where(f == 0, jnp.concatenate([a, b]), jnp.concatenate([b, a]))

    upper = in_order(sent[:rank_part], came[:rank_part]) * BF16(ADAPTER_SCALE)
    lower_o = in_order(sent[rank_part:], came[rank_part:]) * BF16(ADAPTER_SCALE)

    message = with_largest_in_reach(cache_lengths, cache_values[:, 0], output_upper_factor)
    bound = jnp.maximum(message[-16:], swap(message[-16:]))

    hidden, message = lax.optimization_barrier((hidden_in, message))
    flat = hidden.reshape(tall, width)
    inputs32 = flat.astype(F32)
    mean_square = jnp.mean(inputs32 * inputs32, axis=-1, keepdims=True)
    normed = (inputs32 * lax.rsqrt(mean_square + NORM_EPS) * input_gain.astype(F32)).astype(BF16)
    mine = lax.dynamic_slice_in_dim(normed, f * half, half, 1)
    theirs = swap(lax.dynamic_slice_in_dim(normed, (1 - f) * half, half, 1))

    message = jnp.concatenate([message[:-16], bound], axis=0)
    message, lower_near = lax.optimization_barrier((message, lower_near))
    upper_o = along_z_far_first(along_y(message))
    bound = jnp.max(upper_o[:, :, -16:]).astype(F32)

    weight_q, _ = lax.optimization_barrier((query_base_weight, lower_near))
    weight_q = fetch(weight_q, "fetch_query")
    half_done = query_project(0, t[None], lower_near, upper, weight_q, mine, theirs)
    query_effective, own, other = query_project(
        1, t[None], lower_far, upper, weight_q, mine, theirs, half_done
    )
    other = swap(other)

    inverse = ROPE_BASE ** (-(np.arange(head_dim // 2) * 2.0) / head_dim)
    inverse = jnp.asarray(inverse.astype(np.float32))
    positions = cache_lengths[:, None] - steps + jnp.arange(steps, dtype=jnp.int32)[None, :]
    angles = positions.astype(F32).reshape(tall, 1) * inverse
    cosine, sine = jnp.cos(angles), jnp.sin(angles)
    context = attend(
        cache_lengths,
        own,
        other,
        query_bias[None, :],
        jnp.concatenate([cosine, cosine], axis=1),
        jnp.concatenate([-sine, sine], axis=1),
        cache_keys[:, 0],
        cache_values[:, 0],
        steps,
        width ** (-0.5),
    )

    output_effective, own, other = output_project(
        t[None], lower_o, upper_o, output_base_weight, context, swap(context)
    )

    small = 2.0**-16
    unit = jnp.maximum(bound, 1e-30) * small
    shrink_by = 1.0 / unit

    def shrink(value):
        return (value * shrink_by) * (features ** (-0.5) * small)

    near, far = reduce_blocks(own, other, shrink)

    near = along_z_far_first(near)
    near = jnp.stack([near, hop(near, 1)], axis=1)
    far = along_z(far)
    near = near.reshape((2 * outer,) + near.shape[2:]).astype(F32)
    far = far.reshape((2 * outer,) + far.shape[2:]).astype(F32)

    residual, normed_out = finish(
        place, jnp.maximum(bound, 1e-30)[None], flat, post_gain[None, :], near, far
    )
    return (
        residual.reshape(hidden_in.shape),
        normed_out.reshape(hidden_in.shape),
        query_effective,
        output_effective,
    )


def solution(mesh):
    in_specs = (
        P(("groups", "fsdp"), None, None),
        P(),
        P(),
        P("fsdp", "tp"),
        P("tp"),
        P("tp", "fsdp"),
        P(("fsdp", "tp"), None),
        P("fsdp", "tp"),
        P("tp", "fsdp"),
        P(None, ("fsdp", "tp")),
        P(("groups", "fsdp"), "tp", None, None),
        P(("groups", "fsdp"), "tp", None, None),
        P(("groups", "fsdp")),
    )
    out_specs = (
        P(("groups", "fsdp"), None, None),
        P(("groups", "fsdp"), None, None),
        P(("groups", "fsdp"), "tp"),
        P(("groups", "tp"), "fsdp"),
    )
    return jax.shard_map(local, mesh=mesh, in_specs=in_specs, out_specs=out_specs, check_vma=False)
```

```python
import functools

import jax
import jax.numpy as jnp
import numpy as np
from jax import lax
from jax.experimental import pallas as pl
from jax.experimental.pallas import tpu as pltpu
from jax.sharding import PartitionSpec as P

NORM_EPS = 1e-06
ROPE_BASE = 1000000.0
ADAPTER_SCALE = 0.5
MIB = 1024 * 1024
BF16 = jnp.bfloat16
F16 = jnp.float16
F32 = jnp.float32
SWAP = [(0, 1), (1, 0)]


def params(room):
    return pltpu.CompilerParams(vmem_limit_bytes=room * MIB)


def cost(flops, read):
    return pl.CostEstimate(flops=flops, bytes_accessed=read, transcendentals=0)


def hop(value, distance):
    total = lax.axis_size("tp")
    return lax.ppermute(value, "tp", [(i, i ^ distance) for i in range(total)])


def swap(value):
    return lax.ppermute(value, "fsdp", SWAP)


def contract_first(left, right):
    return lax.dot_general(left, right, (((0,), (0,)), ((), ())), preferred_element_type=F32)


VMEM = pl.BlockSpec(memory_space=pltpu.VMEM)
SMEM = pl.BlockSpec(memory_space=pltpu.SMEM)
ANY = pl.BlockSpec(memory_space=pl.ANY)


def in_vmem(value):
    return pltpu.with_memory_space_constraint(value, pltpu.VMEM)


def in_hbm(value):
    return pltpu.with_memory_space_constraint(value, pltpu.HBM)


def fetch_kernel(source, target, arrived):
    copy = pltpu.make_async_copy(source, target, arrived)
    copy.start()
    copy.wait()


def fetch(value, name):
    return pl.pallas_call(
        fetch_kernel,
        in_specs=[ANY],
        out_specs=VMEM,
        out_shape=pltpu.VMEM(value.shape, value.dtype),
        scratch_shapes=[pltpu.SemaphoreType.DMA],
        compiler_params=params(2),
        cost_estimate=cost(0, 2 * value.size),
        name=name,
    )(in_hbm(value))


def reach_kernel(lengths, values, upper, message, held, arrived, factor, factor_arrived):
    rows, slots, head_dim = values.shape
    rank, width = upper.shape
    copies = [
        pltpu.make_async_copy(values.at[row], held.at[row], arrived.at[row]) for row in range(rows)
    ]
    columns = pltpu.make_async_copy(upper, factor, factor_arrived)
    columns.start()
    for copy in copies:
        copy.start()
    part = 256
    slot = lax.broadcasted_iota(jnp.int32, (part, head_dim), 0)
    top = jnp.zeros((16, head_dim), BF16)
    edge = jnp.zeros((8, head_dim), F32)
    for row in range(rows):
        copies[row].wait()
        whole = lengths[row] // part

        def full(n, top, row=row):
            size = jnp.abs(held[row, pl.ds(pl.multiple_of(n * part, part), part)])
            return jnp.maximum(top, jnp.max(size.reshape(-1, 16, head_dim), axis=0))

        top = lax.fori_loop(0, whole, full, top)
        last = pl.multiple_of(jnp.minimum(whole, slots // part - 1) * part, part)
        size = jnp.abs(held[row, pl.ds(last, part)].astype(F32))
        size = jnp.where(slot < lengths[row] - last, size, 0.0)
        edge = jnp.maximum(edge, jnp.max(size.reshape(-1, 8, head_dim), axis=0))
    most = jnp.maximum(jnp.max(top.astype(F32)), jnp.max(edge))
    columns.wait()
    for first in range(0, width, 128):
        message[first // 128 * rank : (first // 128 + 1) * rank] = factor[:, first : first + 128]
    message[width // 128 * rank :] = jnp.broadcast_to(most, (16, 128)).astype(BF16)


def with_largest_in_reach(lengths, values, upper):
    rank, width = upper.shape
    return pl.pallas_call(
        reach_kernel,
        in_specs=[SMEM, ANY, ANY],
        out_specs=VMEM,
        out_shape=jax.ShapeDtypeStruct((width // 128 * rank + 16, 128), BF16),
        scratch_shapes=[
            pltpu.VMEM(values.shape, BF16),
            pltpu.SemaphoreType.DMA((values.shape[0],)),
            pltpu.VMEM(upper.shape, BF16),
            pltpu.SemaphoreType.DMA,
        ],
        compiler_params=params(8),
        cost_estimate=cost(4 * values.size, 2 * values.size),
        name="with_largest_in_reach",
    )(lengths, in_hbm(values), in_hbm(upper))


def query_kernel(y, place, lower, upper, base, mine, theirs, *refs):
    before, (effective, own, other, fresh, total, left) = refs[: 3 * y], refs[3 * y :]
    outer, _, depth = lower.shape
    rows = mine.shape[0]
    if y:
        total[:rows] = before[1][...]
        total[rows:] = before[2][...]
    else:
        total[...] = jnp.zeros_like(total)

    def pair(half, _):
        for slot in range(2):
            z = 2 * half + slot
            start = pl.multiple_of(((2 * z + y) ^ place[0]) * depth, depth)
            block = pl.ds(start, depth)
            out = pltpu.make_async_copy(fresh.at[slot], effective.at[block], left.at[slot])

            @pl.when(half > 0)
            def _():
                out.wait()

            update = contract_first(lower[z], upper[...])
            fresh[slot] = (base[block, :].astype(F32) + update).astype(BF16)
            out.start()
            both = jnp.concatenate([mine[:, block], theirs[:, block]], axis=0)
            total[...] += jnp.dot(both, fresh[slot], preferred_element_type=F32)
        return 0

    lax.fori_loop(0, outer // 2, pair, 0)
    own[...] = total[:rows]
    other[...] = total[rows:]
    for slot in range(2):
        pltpu.make_async_copy(
            fresh.at[slot], effective.at[pl.ds(0, depth)], left.at[slot]
        ).wait()


def query_project(y, place, lower, upper, base, mine, theirs, before=()):
    depth = lower.shape[2]
    width = base.shape[1]
    rows = mine.shape[0]
    return pl.pallas_call(
        functools.partial(query_kernel, y),
        in_specs=[SMEM] + [VMEM] * 5 + [ANY, VMEM, VMEM][: len(before)],
        out_specs=[ANY, VMEM, VMEM],
        out_shape=[
            jax.ShapeDtypeStruct(base.shape, BF16),
            jax.ShapeDtypeStruct((rows, width), F32),
            jax.ShapeDtypeStruct((rows, width), F32),
        ],
        scratch_shapes=[
            pltpu.VMEM((2, depth, width), BF16),
            pltpu.VMEM((2 * rows, width), F32),
            pltpu.SemaphoreType.DMA((2,)),
        ],
        input_output_aliases={6: 0} if before else {},
        compiler_params=params(14),
        cost_estimate=cost(base.size * (lower.shape[1] + 2 * rows), base.size),
        name="query_project",
    )(place, lower, upper, in_vmem(base), mine, theirs, *before)


def attend_kernel(
    steps, scale, lengths, own, other, bias, cosine, sine, keys, values, context,
    keys_held, values_held, arrived
):
    rows, slots, head_dim = keys.shape
    heads = own.shape[1] // head_dim
    copies = []
    for row in range(rows):
        copies.append(
            [
                pltpu.make_async_copy(keys.at[row], keys_held.at[row], arrived.at[0, row]),
                pltpu.make_async_copy(values.at[row], values_held.at[row], arrived.at[1, row]),
            ]
        )
        for copy in copies[row]:
            copy.start()
    slot = lax.broadcasted_iota(jnp.int32, (heads * steps, slots), 1)
    step = lax.broadcasted_iota(jnp.int32, (heads * steps, slots), 0) % steps
    behind = slot - step
    many = heads * steps
    nothing = jnp.zeros((many, head_dim), F32)
    for first in range(0, rows, 2):
        pair = (first, first + 1)
        span = slice(first * steps, (first + 2) * steps)
        query = (own[span] + other[span]) * scale + bias[...].astype(F32)
        turned = []
        for head in range(heads):
            part = query[:, head * head_dim : (head + 1) * head_dim]
            part = part * cosine[span] + pltpu.roll(part, head_dim // 2, 1) * sine[span]
            turned.append(part * head_dim ** (-0.5))
        upper, lower = [
            jnp.concatenate([q[i * steps : (i + 1) * steps] for q in turned], axis=0) for i in (0, 1)
        ]
        queries = jnp.concatenate(
            [
                jnp.concatenate([upper, nothing], axis=1),
                jnp.concatenate([nothing, lower], axis=1),
            ],
            axis=0,
        ).astype(BF16)
        for row in pair:
            copies[row][0].wait()
        both = jnp.concatenate([keys_held[row] for row in pair], axis=1)
        scores = lax.dot_general(
            queries, both, (((1,), (1,)), ((), ())), preferred_element_type=F32
        )
        scores = jnp.concatenate(
            [
                jnp.where(
                    behind <= lengths[first + i] - steps,
                    scores[i * many : (i + 1) * many],
                    F32(-1e30),
                )
                for i in (0, 1)
            ],
            axis=0,
        )
        top = jnp.max(scores, axis=-1, keepdims=True)
        weights = jnp.exp(scores - top)
        probs = (weights / jnp.sum(weights, axis=-1, keepdims=True)).astype(BF16)
        for row in pair:
            copies[row][1].wait()
        both = jnp.concatenate([values_held[row] for row in pair], axis=1)
        mixed = jnp.dot(probs, both, preferred_element_type=F32)
        gathered = (mixed[:many, :head_dim], mixed[many:, head_dim:])
        for head in range(heads):
            context[span, head * head_dim : (head + 1) * head_dim] = jnp.concatenate(
                [g[head * steps : (head + 1) * steps] for g in gathered], axis=0
            ).astype(BF16)


def attend(lengths, own, other, bias, cosine, sine, keys, values, steps, scale):
    rows = keys.shape[0]
    width = own.shape[1]
    return pl.pallas_call(
        functools.partial(attend_kernel, steps, scale),
        in_specs=[SMEM] + [VMEM] * 5 + [ANY] * 2,
        out_specs=VMEM,
        out_shape=jax.ShapeDtypeStruct((rows * steps, width), BF16),
        scratch_shapes=[
            pltpu.VMEM(keys.shape, BF16),
            pltpu.VMEM(values.shape, BF16),
            pltpu.SemaphoreType.DMA((2, rows)),
        ],
        compiler_params=params(18),
        cost_estimate=cost(4 * keys.size * width // keys.shape[2] * steps, 4 * keys.size),
        name="attend",
    )(lengths, own, other, bias, cosine, sine, in_hbm(keys), in_hbm(values))


def output_kernel(
    place, lower, upper, base, mine, theirs, effective, own, other, held, fresh, arrived, left
):
    outer = upper.shape[0]
    rank = lower.shape[0]
    width = fresh.shape[2]
    rows = mine.shape[0]

    def columns(k):
        return pl.ds(pl.multiple_of((k ^ place[0]) * width, width), width)

    def fetch(k):
        return pltpu.make_async_copy(base.at[:, columns(k)], held.at[k], arrived.at[k])

    def ask(k, _):
        fetch(k).start()
        return 0

    lax.fori_loop(0, 2 * outer, ask, 0)
    both = jnp.concatenate([mine[...], theirs[...]], axis=0)

    def pair(z, _):
        for y in range(2):
            k = 2 * z + y
            out = pltpu.make_async_copy(fresh.at[y], effective.at[:, columns(k)], left.at[y])

            @pl.when(z > 0)
            def _():
                out.wait()

            factor = [upper[lax.rem(outer - z, outer), y, n * rank : (n + 1) * rank] for n in range(width // 128)]
            update = contract_first(lower[...], jnp.concatenate(factor, axis=1))
            fetch(k).wait()
            fresh[y] = (held[k].astype(F32) + update).astype(BF16)
            out.start()
            product = jnp.dot(both, fresh[y], preferred_element_type=F32)
            own[y, z] = product[:rows]
            other[z, y] = product[rows:]
        return 0

    lax.fori_loop(0, outer, pair, 0)
    for y in range(2):
        pltpu.make_async_copy(fresh.at[y], effective.at[:, pl.ds(0, width)], left.at[y]).wait()


def output_project(place, lower, upper, base, mine, theirs):
    outer = upper.shape[0]
    width = base.shape[1] // (2 * outer)
    depth = base.shape[0]
    rows = mine.shape[0]
    return pl.pallas_call(
        output_kernel,
        in_specs=[SMEM, VMEM, VMEM, ANY, VMEM, VMEM],
        out_specs=[ANY, VMEM, VMEM],
        out_shape=[
            jax.ShapeDtypeStruct(base.shape, BF16),
            jax.ShapeDtypeStruct((2, outer, rows, width), F32),
            jax.ShapeDtypeStruct((outer, 2, rows, width), F32),
        ],
        scratch_shapes=[
            pltpu.VMEM((2 * outer, depth, width), BF16),
            pltpu.VMEM((2, depth, width), BF16),
            pltpu.SemaphoreType.DMA((2 * outer,)),
            pltpu.SemaphoreType.DMA((2,)),
        ],
        compiler_params=params(24),
        cost_estimate=cost(2 * base.size * (lower.shape[0] + 2 * rows), 4 * base.size),
        name="output_project",
    )(place, lower, upper, in_hbm(base), mine, theirs)


def finish_kernel(place, bound, hidden, gain, near, far, residual, normed, combined, held, left):
    blocks, rows, width = near.shape
    half = blocks * width
    tall = combined.shape[0]

    def put(which, out, first):
        slot = first // tall % 2
        return pltpu.make_async_copy(
            held.at[which, slot], out.at[pl.ds(first, tall)], left.at[which, slot]
        )

    for first in range(0, rows, tall):
        slot = first // tall % 2
        if first >= 2 * tall:
            put(0, residual, first - 2 * tall).wait()
            put(1, normed, first - 2 * tall).wait()
        squares = jnp.zeros((tall, 128), F32)
        for pieces, which in ((near, place[1]), (far, 1 - place[1])):
            for k in range(blocks):
                at = (blocks - k // 2 * 2) % blocks + k % 2 if pieces is near else k
                start = pl.multiple_of(which * half + (place[0] ^ at) * width, width)
                total = hidden[first : first + tall, pl.ds(start, width)].astype(F32)
                total += pieces[k, first : first + tall] * bound[0]
                combined[:, pl.ds(start, width)] = total
                held[0, slot, :, pl.ds(start, width)] = total.astype(BF16)
                for lane in range(0, width, 128):
                    squares += total[:, lane : lane + 128] * total[:, lane : lane + 128]
        put(0, residual, first).start()
        mean = jnp.sum(squares, axis=-1, keepdims=True) / (2 * half)
        inverse = lax.rsqrt(mean + NORM_EPS)
        held[1, slot] = (combined[...] * inverse * gain[...].astype(F32)).astype(BF16)
        put(1, normed, first).start()
    for first in range(max(rows - 2 * tall, 0), rows, tall):
        put(0, residual, first).wait()
        put(1, normed, first).wait()


def finish(place, bound, hidden, gain, near, far):
    rows, whole = hidden.shape
    tall = 32
    return pl.pallas_call(
        finish_kernel,
        in_specs=[SMEM, SMEM] + [VMEM] * 4,
        out_specs=[ANY, ANY],
        out_shape=[jax.ShapeDtypeStruct((rows, whole), BF16)] * 2,
        scratch_shapes=[
            pltpu.VMEM((tall, whole), F32),
            pltpu.VMEM((2, 2, tall, whole), BF16),
            pltpu.SemaphoreType.DMA((2, 2)),
        ],
        compiler_params=params(14),
        cost_estimate=cost(8 * hidden.size, 14 * hidden.size),
        name="finish",
    )(place, bound, hidden, gain, near, far)


def cross(value):
    total = lax.axis_size("tp")
    pairs = [(f * total + i, (1 - f) * total + (i ^ 1)) for f in range(2) for i in range(total)]
    return lax.ppermute(value, ("fsdp", "tp"), pairs)


def along_z(value):
    outer = lax.axis_size("tp") // 2
    return jnp.stack([value] + [hop(value, 2 * k) for k in range(1, outer)])


def along_z_far_first(value):
    outer = lax.axis_size("tp") // 2
    return jnp.stack([value] + [hop(value, 2 * k) for k in range(outer - 1, 0, -1)])


def along_y(value):
    return jnp.stack([value, hop(value, 1)])


def reduce_blocks(own, other, shrink):
    outer = other.shape[0]

    def narrow(value):
        return value.astype(F16)

    across = hop(narrow(shrink(own[1])), 1)
    arrived = [hop(narrow(shrink(other[k])), 2 * k) for k in range(outer - 1, 0, -1)]
    summed = shrink(own[0]) + across.astype(F32)
    ended = [hop(narrow(summed[k]), 2 * k) for k in range(1, outer)]
    arrived, ended[:1] = lax.optimization_barrier((arrived, ended[:1]))
    total = summed[0] + sum(e.astype(F32) for e in ended)
    pair = narrow(shrink(other[0]) + sum(a.astype(F32) for a in arrived))
    far = swap(pair).astype(F32) + cross(pair)[::-1].astype(F32)
    return narrow(total), narrow(far)


def local(
    hidden_in,
    input_gain,
    post_gain,
    query_base_weight,
    query_bias,
    output_base_weight,
    query_lower_factor,
    query_upper_factor,
    output_lower_factor,
    output_upper_factor,
    cache_keys,
    cache_values,
    cache_lengths,
):
    rows, steps, width = hidden_in.shape
    tall = rows * steps
    half = width // 2
    slots, head_dim = cache_keys.shape[2:]
    features = query_base_weight.shape[1] * lax.axis_size("tp")
    t = lax.axis_index("tp").astype(jnp.int32)
    f = lax.axis_index("fsdp").astype(jnp.int32)
    place = jnp.stack([t, f])
    outer = lax.axis_size("tp") // 2

    lower_near = along_z(query_lower_factor.T)
    lower_far = hop(lower_near, 1)

    rank_part = query_upper_factor.shape[0]
    sent = jnp.concatenate([query_upper_factor, output_lower_factor.T], axis=0)
    came = swap(sent)

    def in_order(a, b):
        return jnp.where(f == 0, jnp.concatenate([a, b]), jnp.concatenate([b, a]))

    upper = in_order(sent[:rank_part], came[:rank_part]) * BF16(ADAPTER_SCALE)
    lower_o = in_order(sent[rank_part:], came[rank_part:]) * BF16(ADAPTER_SCALE)

    message = with_largest_in_reach(cache_lengths, cache_values[:, 0], output_upper_factor)
    bound = jnp.maximum(message[-16:], swap(message[-16:]))

    hidden, message = lax.optimization_barrier((hidden_in, message))
    flat = hidden.reshape(tall, width)
    inputs32 = flat.astype(F32)
    mean_square = jnp.mean(inputs32 * inputs32, axis=-1, keepdims=True)
    normed = (inputs32 * lax.rsqrt(mean_square + NORM_EPS) * input_gain.astype(F32)).astype(BF16)
    mine = lax.dynamic_slice_in_dim(normed, f * half, half, 1)
    theirs = swap(lax.dynamic_slice_in_dim(normed, (1 - f) * half, half, 1))

    message = jnp.concatenate([message[:-16], bound], axis=0)
    message, lower_near = lax.optimization_barrier((message, lower_near))
    upper_o = along_z_far_first(along_y(message))
    bound = jnp.max(upper_o[:, :, -16:]).astype(F32)

    weight_q, _ = lax.optimization_barrier((query_base_weight, lower_near))
    weight_q = fetch(weight_q, "fetch_query")
    half_done = query_project(0, t[None], lower_near, upper, weight_q, mine, theirs)
    query_effective, own, other = query_project(
        1, t[None], lower_far, upper, weight_q, mine, theirs, half_done
    )
    other = swap(other)

    inverse = ROPE_BASE ** (-(np.arange(head_dim // 2) * 2.0) / head_dim)
    inverse = jnp.asarray(inverse.astype(np.float32))
    positions = cache_lengths[:, None] - steps + jnp.arange(steps, dtype=jnp.int32)[None, :]
    angles = positions.astype(F32).reshape(tall, 1) * inverse
    cosine, sine = jnp.cos(angles), jnp.sin(angles)
    context = attend(
        cache_lengths,
        own,
        other,
        query_bias[None, :],
        jnp.concatenate([cosine, cosine], axis=1),
        jnp.concatenate([-sine, sine], axis=1),
        cache_keys[:, 0],
        cache_values[:, 0],
        steps,
        width ** (-0.5),
    )

    output_effective, own, other = output_project(
        t[None], lower_o, upper_o, output_base_weight, context, swap(context)
    )

    small = 2.0**-16
    unit = jnp.maximum(bound, 1e-30) * small
    shrink_by = 1.0 / unit

    def shrink(value):
        return (value * shrink_by) * (features ** (-0.5) * small)

    near, far = reduce_blocks(own, other, shrink)

    near = along_z_far_first(near)
    near = jnp.stack([near, hop(near, 1)], axis=1)
    far = along_z(far)
    near = near.reshape((2 * outer,) + near.shape[2:]).astype(F32)
    far = far.reshape((2 * outer,) + far.shape[2:]).astype(F32)

    residual, normed_out = finish(
        place, jnp.maximum(bound, 1e-30)[None], flat, post_gain[None, :], near, far
    )
    return (
        residual.reshape(hidden_in.shape),
        normed_out.reshape(hidden_in.shape),
        query_effective,
        output_effective,
    )


def solution(mesh):
    in_specs = (
        P(("groups", "fsdp"), None, None),
        P(),
        P(),
        P("fsdp", "tp"),
        P("tp"),
        P("tp", "fsdp"),
        P(("fsdp", "tp"), None),
        P("fsdp", "tp"),
        P("tp", "fsdp"),
        P(None, ("fsdp", "tp")),
        P(("groups", "fsdp"), "tp", None, None),
        P(("groups", "fsdp"), "tp", None, None),
        P(("groups", "fsdp")),
    )
    out_specs = (
        P(("groups", "fsdp"), None, None),
        P(("groups", "fsdp"), None, None),
        P(("groups", "fsdp"), "tp"),
        P(("groups", "tp"), "fsdp"),
    )
    return jax.shard_map(local, mesh=mesh, in_specs=in_specs, out_specs=out_specs, check_vma=False)
```
